256 devices in a mesh: slot: 16 (over y, x), row: 16 (over z, core).
Axes of the slice: x: 4, y: 4, z: 8, core: 2. Of those that a mesh axis runs over, the one named last changes fastest.
Arguments:
- innovation: bfloat16 [16, 3, 1408, 1408], P('slot', None, 'row'), may hold values from -6 to 6
- clear_mask: int32 [16, 3, 1408, 1408], P('slot', None, 'row'), may hold values 0 or 1
- lag_list: int32 [4], replicated, may hold values from 0 to 15, as said below
Outputs:
- cross_spectra: float32 [2, 4, 3, 1408, 1408], P(None, None, None, 'slot', 'row')
The draws below stay inside these ranges and needn't reach their ends.
Inputs may be any that keep to these rules, and one draw needn't show every extreme that they name: `lag_list`: both 0 and 15 appear in every list; entries may repeat.
All inputs are finite; a program needn't handle non-finite values. No bound on the sum of `clear_mask` on one device may be relied on, other than what follows from the above.
Results may differ from the reference program's by a relative error of at most 0.009.
Values may be sent and summed in bfloat16 or wider, within the bound.
No kernel may reach another device: no remote copies, remote signals or barrier semaphores. Data moves between devices by JAX's collectives and lax.ppermute only.
A program may use at most 128 MiB of HBM per device.

```python
import math
import jax
import jax.numpy as jnp
from jax import lax

R = 1408
C = 1408
CH = 3
LAGS = 4
SLOTS = 16


def draw_lag_list(key, part):
    key = jax.random.fold_in(key, 7)
    first_key, second_key, third_key = jax.random.split(key, 3)
    values = jax.random.randint(first_key, (LAGS,), 0, SLOTS)
    top_at = jax.random.randint(second_key, (), 0, LAGS)
    zero_at = (top_at + 1 + jax.random.randint(third_key, (), 0, LAGS - 1)) % LAGS
    positions = jnp.arange(LAGS)
    values = jnp.where(positions == top_at, SLOTS - 1, values)
    values = jnp.where(positions == zero_at, 0, values)
    return values.astype(jnp.int32)


def plant(array, own_key, low, top_value):
    longest = array.shape.index(max(array.shape))
    spots = []
    for shift in (0, 1):
        where = [jax.random.randint(jax.random.fold_in(own_key, axis), (), 0, length) for axis, length in enumerate(array.shape)]
        where[longest] = (where[longest] + shift) % array.shape[longest]
        spots.append(tuple(where))
    return array.at[spots[0]].set(low).at[spots[1]].set(top_value)


def shard_levels(key, extent, shards, least, largest):
    def one(axis_at, parts):
        draws = jax.random.uniform(jax.random.fold_in(jax.random.fold_in(key, 6), axis_at), (parts,), jnp.float32, least / len(shards), largest / len(shards))
        return jnp.repeat(jnp.exp(draws), extent[axis_at] // parts).reshape((-1,) + (1,) * (len(extent) - axis_at - 1))

    loudness = one(*shards[0])
    for cut in shards[1:]:
        loudness = loudness * one(*cut)
    return loudness


def centred(key, shape, deviation, reach, cuts=(), kind=jnp.bfloat16):
    entries = jax.random.normal(key, shape, jnp.float32) * deviation
    if len(cuts) > 0:
        entries = shard_levels(key, shape, cuts, -0.22, 0.18) * entries
    return jnp.clip(entries, min=-reach, max=reach).astype(kind)


def setup_inputs(seed: int = 0) -> dict:
    arg_keys = jax.random.split(jax.random.key(seed), 4)
    innovation = centred(arg_keys[0], (SLOTS, CH, R, C), 1.0, 6.0, ((0, 16), (2, 16)))
    clear_mask = plant((jax.random.randint(arg_keys[1], (SLOTS, CH, R, C), 0, 4) < 3).astype(jnp.int32), jax.random.fold_in(arg_keys[1], 1), 0, 1)
    lag_list = draw_lag_list(jax.random.fold_in(arg_keys[3], 71), 0)
    return dict(innovation=innovation, clear_mask=clear_mask, lag_list=lag_list)


def tables(length):
    indices = jnp.arange(length, dtype=jnp.int32)
    phases = indices[:, None] * indices[None, :] % length
    angles = phases.astype(jnp.float32) * (2.0 * math.pi / length)
    norm_scale = 1.0 / math.sqrt(length)
    return ((jnp.cos(angles) * norm_scale).astype(jnp.bfloat16), (jnp.sin(angles) * norm_scale).astype(jnp.bfloat16))

def spectrum(masked, cosine_cols, sine_cols, cosine_rows, sine_rows):
    flattened = masked.reshape(-1, C)
    g_real = jnp.dot(flattened, cosine_cols, preferred_element_type=jnp.float32).astype(jnp.bfloat16).reshape(CH, R, C)
    g_imag = (-jnp.dot(flattened, sine_cols, preferred_element_type=jnp.float32)).astype(jnp.bfloat16).reshape(CH, R, C)
    cos_wide = cosine_rows.astype(jnp.float32)
    sin_wide = sine_rows.astype(jnp.float32)
    real_wide = g_real.astype(jnp.float32)
    imag_wide = g_imag.astype(jnp.float32)
    f_real = jnp.einsum('kr,crq->ckq', cos_wide, real_wide) + jnp.einsum('kr,crq->ckq', sin_wide, imag_wide)
    f_imag = jnp.einsum('kr,crq->ckq', cos_wide, imag_wide) - jnp.einsum('kr,crq->ckq', sin_wide, real_wide)
    return jnp.stack([f_real, f_imag]).astype(jnp.bfloat16)

def reference(innovation, clear_mask, lag_list):
    masked = innovation * clear_mask.astype(jnp.bfloat16)
    cosine_cols, sine_cols = tables(C)
    cosine_rows, sine_rows = tables(R)
    spectra = lax.map(lambda slab: spectrum(slab, cosine_cols, sine_cols, cosine_rows, sine_rows), masked)

    def lag_sum(lag_value):
        lag_value = lag_value.astype(jnp.int32)

        def accumulate(slot_index, running):
            slot_index = jnp.asarray(slot_index).astype(jnp.int32)
            later_index = jnp.minimum(slot_index + lag_value, SLOTS - 1).astype(jnp.int32)
            earlier = lax.dynamic_index_in_dim(spectra, slot_index, 0, keepdims=False).astype(jnp.float32)
            later = lax.dynamic_index_in_dim(spectra, later_index, 0, keepdims=False).astype(jnp.float32)
            pair_real = earlier[0] * later[0] + earlier[1] * later[1]
            pair_imag = earlier[1] * later[0] - earlier[0] * later[1]
            rounded = lax.optimization_barrier(jnp.stack([pair_real, pair_imag]).astype(jnp.bfloat16)).astype(jnp.float32)
            inside = slot_index + lag_value < SLOTS
            return running + jnp.where(inside, rounded, jnp.zeros_like(rounded))
        summed = lax.fori_loop(0, SLOTS, accumulate, jnp.zeros((2, CH, R, C), jnp.float32))
        return summed / (SLOTS - lag_value).astype(jnp.float32)
    results = lax.map(lag_sum, lag_list)
    return jnp.transpose(results, (1, 0, 2, 3, 4))
```

```python
import functools
import math

import jax
import jax.numpy as jnp
import ml_dtypes
import numpy as np
from jax import lax
from jax.experimental import pallas as pl
from jax.experimental.pallas import tpu as pltpu
from jax.sharding import PartitionSpec as P

F32 = jnp.float32
BF16 = jnp.bfloat16
LANES = 128
GROUP = 16


def phase(numbers, length):
    return (numbers % length) * (2.0 * math.pi / length)


def column_table(length, parts, half, width):
    block = length // parts
    kx = (np.arange(parts)[:, None] * block + np.arange(half)[None, :]) % length
    angles = phase(np.arange(length)[:, None, None] * kx[None], length)
    table = np.zeros((length, parts, LANES))
    table[:, :, :half] = np.cos(angles)
    table[:, :, half:width] = -np.sin(angles)
    return (table / math.sqrt(length)).reshape(length, parts * LANES).astype(ml_dtypes.bfloat16)


def row_table(length, parts, rows_up, row_order):
    block = length // parts
    ky = np.arange(parts // 2)[:, None] * block + np.arange(block + 1)[None, :]
    angles = phase(ky[:, :, None] * row_order[None, None, :], length)
    table = np.zeros((parts // 2, 2, rows_up, row_order.size))
    table[:, 0, : block + 1] = np.cos(angles)
    table[:, 1, : block + 1] = np.sin(angles)
    return (table / math.sqrt(length)).reshape(-1, row_order.size).astype(ml_dtypes.bfloat16)


def lane_index(shape):
    return lax.broadcasted_iota(jnp.int32, shape, len(shape) - 1)


def pack(groups, width, tiles):
    lane = lane_index((GROUP, LANES))
    out = [None] * tiles

    def put(tile, value):
        out[tile] = value if out[tile] is None else out[tile] + value

    for number, value in enumerate(groups):
        tile, shift = divmod(number * width, LANES)
        if shift:
            value = pltpu.roll(value, shift, 1)
        if shift + width <= LANES:
            put(tile, value)
        else:
            put(tile, jnp.where(lane >= shift, value, 0.0))
            put(tile + 1, jnp.where(lane < shift, value, 0.0))
    return jnp.concatenate(out, axis=1)


def unpack(load, number, width, rows):
    lane = lane_index((rows, LANES))
    tile, shift = divmod(number * width, LANES)
    value = load(tile)
    if shift + width > LANES:
        value = jnp.where(lane >= shift, value, load(tile + 1))
    if shift:
        value = pltpu.roll(value, LANES - shift, 1)
    return jnp.where(lane < width, value, 0.0)


def column_kernel(width, x_ref, mask_ref, table_ref, out_ref, left):
    channels, rows = x_ref.shape[1], x_ref.shape[2]
    whole = rows // GROUP * GROUP

    @pl.when(pl.program_id(0) == 0)
    def _():
        masked = [x_ref[0, c].astype(F32) * mask_ref[0, c].astype(F32) for c in range(channels)]
        pieces = [value[:whole] for value in masked] + [value[whole:] for value in masked]
        used = channels * rows
        if left.shape[0] > used:
            pieces.append(jnp.zeros((left.shape[0] - used, left.shape[1]), F32))
        left[...] = jnp.concatenate(pieces, axis=0).astype(BF16)

    result = jnp.dot(left[...], table_ref[...], preferred_element_type=F32)
    for part in range(out_ref.shape[0]):
        lanes = slice(part * LANES, (part + 1) * LANES)
        groups = [result[g * GROUP : (g + 1) * GROUP, lanes] for g in range(left.shape[0] // GROUP)]
        out_ref[part] = pack(groups, width, out_ref.shape[2] // LANES).astype(BF16)


def row_kernel(width, channels, rows_up, x_ref, table_ref, out_ref, right):
    half = width // 2
    parts = x_ref.shape[0]
    depth = parts * GROUP
    steps = right.shape[0] // depth
    step = pl.program_id(0)

    @pl.when(step == 0)
    def _():
        def load(tile):
            return x_ref[:, :, tile * LANES : (tile + 1) * LANES].reshape(depth, LANES).astype(F32)

        row_in_group = lax.broadcasted_iota(jnp.int32, (depth, LANES), 0) % GROUP
        for c in range(channels):
            lanes = slice(c * LANES, (c + 1) * LANES)
            for a in range(steps - 1):
                value = unpack(load, c * (steps - 1) + a, width, depth)
                right[a * depth : (a + 1) * depth, lanes] = value.astype(BF16)
            value = unpack(load, channels * (steps - 1) + c // 2, width, depth)
            value = jnp.where((row_in_group >= GROUP // 2) == (c % 2 == 1), value, 0.0)
            right[(steps - 1) * depth :, lanes] = value.astype(BF16)

    result = jnp.dot(table_ref[...], right[...], preferred_element_type=F32)
    lane = lane_index((rows_up, LANES))
    blocks = table_ref.shape[0] // (2 * rows_up)
    for b in range(blocks):
        plus, minus = [], []
        for c in range(channels):
            lanes = slice(c * LANES, (c + 1) * LANES)
            top = 2 * b * rows_up
            even = result[top : top + rows_up, lanes]
            odd = result[top + rows_up : top + 2 * rows_up, lanes]
            turned = jnp.where(
                lane < half,
                pltpu.roll(odd, LANES - half, 1),
                jnp.where(lane < width, -pltpu.roll(odd, half, 1), 0.0),
            )
            plus.append(even + turned)
            minus.append(even - turned)
        for value, place in ((plus, step * blocks + b), (minus, parts - 1 - step * blocks - b)):
            groups = [v[a : a + GROUP] for v in value for a in range(0, rows_up, GROUP)]
            out_ref[place] = pack(groups, width, out_ref.shape[2] // LANES).astype(BF16)


def lag_kernel(half, lag_ref, z_ref, first_ref, out_ref, wide, swapped):
    slots, rows, lanes = z_ref.shape
    first = first_ref[...] > 0.0

    def swap(value):
        return jnp.where(first, pltpu.roll(value, lanes - half, 1), pltpu.roll(value, half, 1))

    for t in range(slots):
        value = z_ref[t].astype(F32)
        wide[t] = value
        swapped[t] = swap(value)
    for entry in range(out_ref.shape[0]):
        lag = lag_ref[entry]

        def add(t, sums):
            later = wide[t + lag]
            return sums[0] + wide[t] * later, sums[1] + swapped[t] * later

        zero = jnp.zeros((rows, lanes), F32)
        real, imag = lax.fori_loop(0, slots - lag, add, (zero, zero))
        value = jnp.where(first, real + swap(real), swap(imag) - imag)
        out_ref[entry] = (value / (slots - lag).astype(F32)).astype(BF16)


def place_kernel(width, channels, rows_up, own_ref, other_ref, spread_ref, out_ref):
    block = out_ref.shape[3]
    per = rows_up // GROUP
    at_row = lax.broadcasted_iota(jnp.int32, (rows_up, rows_up), 0)
    at_col = lax.broadcasted_iota(jnp.int32, (rows_up, rows_up), 1)
    back = lax.axis_index("slot") * 2 >= lax.axis_size("slot")
    source = jnp.where(back, block - at_row, at_row)
    order = (source == at_col).astype(F32).astype(BF16)
    for entry in range(out_ref.shape[1]):
        for c in range(channels):
            sides = []
            for ref in (own_ref, other_ref):
                def load(tile):
                    return ref[entry, :, tile * LANES : (tile + 1) * LANES].astype(F32)

                sides.append(
                    jnp.concatenate([unpack(load, c * per + a, width, GROUP) for a in range(per)], axis=0)
                )
            both = jnp.concatenate(sides, axis=1).astype(BF16)
            spread = jnp.dot(both, spread_ref[...], preferred_element_type=F32).astype(BF16)
            placed = jnp.dot(order, spread, preferred_element_type=F32)
            out_ref[0, entry, c] = placed[:block, :block]
            out_ref[1, entry, c] = placed[:block, LANES : LANES + block]


def spread_table(block, half):
    table = np.zeros((2 * LANES, 2 * LANES))
    for j in range(block):
        if j < half:
            table[j, j] = 1.0
            table[half + j, LANES + j] = 1.0
        else:
            table[LANES + block - j, j] = 1.0
            table[LANES + half + block - j, LANES + j] = -1.0
    return table.astype(ml_dtypes.bfloat16)


def up(value, unit):
    return -(-value // unit) * unit


def on_device(slots, parts, innovation, clear_mask, lag_list):
    _, channels, rows, cols = innovation.shape
    length = rows * parts
    block = cols // parts
    half = block // 2 + 1
    width = 2 * half
    entries = lag_list.shape[0]
    limit = pltpu.CompilerParams(vmem_limit_bytes=40 * 2**20)

    left_rows = up(channels * rows, GROUP)
    packed = up(left_rows // GROUP * width, LANES)
    per_step = 4
    g = pl.pallas_call(
        functools.partial(column_kernel, width),
        grid=(parts // per_step,),
        in_specs=[
            pl.BlockSpec(innovation.shape, lambda i: (0, 0, 0, 0)),
            pl.BlockSpec(clear_mask.shape, lambda i: (0, 0, 0, 0)),
            pl.BlockSpec((cols, per_step * LANES), lambda i: (0, i)),
        ],
        out_specs=pl.BlockSpec((per_step, GROUP, packed), lambda i: (i, 0, 0)),
        out_shape=jax.ShapeDtypeStruct((parts, GROUP, packed), BF16),
        scratch_shapes=[pltpu.VMEM((left_rows, cols), BF16)],
        compiler_params=limit,
        name="columns",
    )(innovation, clear_mask, jnp.asarray(column_table(cols, parts, half, width)))
    g = lax.all_to_all(g, "row", 0, 0, tiled=True)

    whole = rows // GROUP
    order = [
        p * rows + (a * GROUP + b if a < whole else whole * GROUP + b % (GROUP // 2))
        for a in range(whole + 1)
        for p in range(parts)
        for b in range(GROUP)
    ]
    ky_block = length // slots
    rows_up = up(ky_block + 1, GROUP)
    table = row_table(length, slots, rows_up, np.array(order))
    packed = up(rows_up // GROUP * channels * width, LANES)
    row_steps = 2
    f = pl.pallas_call(
        functools.partial(row_kernel, width, channels, rows_up),
        grid=(row_steps,),
        in_specs=[
            pl.BlockSpec(g.shape, lambda i: (0, 0, 0)),
            pl.BlockSpec((table.shape[0] // row_steps, table.shape[1]), lambda i: (i, 0)),
        ],
        out_specs=pl.BlockSpec((slots, GROUP, packed), lambda i: (0, 0, 0)),
        out_shape=jax.ShapeDtypeStruct((slots, GROUP, packed), BF16),
        scratch_shapes=[pltpu.VMEM((table.shape[1], channels * LANES), BF16)],
        compiler_params=limit,
        name="rows",
    )(g, jnp.asarray(table))
    f = lax.all_to_all(f, "slot", 0, 0, tiled=True)

    first = np.broadcast_to((np.arange(packed) % width < half).astype(np.float32), (GROUP, packed))
    own = pl.pallas_call(
        functools.partial(lag_kernel, half),
        in_specs=[
            pl.BlockSpec(memory_space=pltpu.SMEM),
            pl.BlockSpec(memory_space=pltpu.VMEM),
            pl.BlockSpec(memory_space=pltpu.VMEM),
        ],
        out_specs=pl.BlockSpec(memory_space=pltpu.VMEM),
        out_shape=jax.ShapeDtypeStruct((entries, GROUP, packed), BF16),
        scratch_shapes=[pltpu.VMEM((slots, GROUP, packed), F32)] * 2,
        compiler_params=limit,
        name="lags",
    )(lag_list, f, jnp.asarray(first))

    mirror = [
        (s * parts + p, (slots - 1 - s) * parts + parts - 1 - p) for s in range(slots) for p in range(parts)
    ]
    other = lax.ppermute(own, ("slot", "row"), mirror)

    return pl.pallas_call(
        functools.partial(place_kernel, width, channels, rows_up),
        in_specs=[pl.BlockSpec(memory_space=pltpu.VMEM)] * 3,
        out_specs=pl.BlockSpec(memory_space=pltpu.VMEM),
        out_shape=jax.ShapeDtypeStruct((2, entries, channels, ky_block, block), F32),
        compiler_params=limit,
        name="place",
    )(own, other, jnp.asarray(spread_table(block, half)))


def solution(mesh):
    placed = (P("slot", None, "row", None), P("slot", None, "row", None), P())
    return jax.shard_map(
        functools.partial(on_device, mesh.shape["slot"], mesh.shape["row"]),
        mesh=mesh,
        in_specs=placed,
        out_specs=P(None, None, None, "slot", "row"),
        check_vma=False,
    )
```

```python
import functools
import math

import jax
import jax.numpy as jnp
import ml_dtypes
import numpy as np
from jax import lax
from jax.experimental import pallas as pl
from jax.experimental.pallas import tpu as pltpu
from jax.sharding import PartitionSpec as P

F32 = jnp.float32
BF16 = jnp.bfloat16
LANES = 128
GROUP = 16


def phase(numbers, length):
    return (numbers % length) * (2.0 * math.pi / length)


def column_table(length, parts, half, pitch, chunks):
    block = length // parts
    kx = (np.arange(parts)[:, None] * block + np.arange(half)[None, :]) % length
    angles = phase(np.arange(length)[:, None, None] * kx[None], length)
    table = np.zeros((length, parts, pitch))
    table[:, :, :half] = np.cos(angles)
    table[:, :, half : 2 * half] = -np.sin(angles)
    table = (table / math.sqrt(length)).reshape(length, chunks, parts // chunks * pitch)
    return np.ascontiguousarray(table.transpose(1, 0, 2)).astype(ml_dtypes.bfloat16)


def row_table(length, parts, rows_up, row_order):
    block = length // parts
    ky = np.arange(parts // 2)[:, None] * block + np.arange(block + 1)[None, :]
    angles = phase(ky[:, :, None] * row_order[None, None, :], length)
    table = np.zeros((parts // 2, 2, rows_up, row_order.size))
    table[:, 0, : block + 1] = np.cos(angles)
    table[:, 1, : block + 1] = np.sin(angles)
    return (table / math.sqrt(length)).reshape(-1, row_order.size).astype(ml_dtypes.bfloat16)


def lane_index(shape):
    return lax.broadcasted_iota(jnp.int32, shape, len(shape) - 1)


class Packed:
    def __init__(self, tiles):
        self.tiles = [jnp.zeros((GROUP, LANES), F32) for _ in range(tiles)]
        self.lane = lane_index((GROUP, LANES))

    def put(self, value, start, width):
        tile, shift = divmod(start, LANES)
        inside = self.lane >= shift
        if shift + width <= LANES:
            inside &= self.lane < shift + width
        else:
            after = self.lane < shift + width - LANES
            self.tiles[tile + 1] = jnp.where(after, value, self.tiles[tile + 1])
        self.tiles[tile] = jnp.where(inside, value, self.tiles[tile])


def turn(value, lanes):
    lanes %= LANES
    return pltpu.roll(value, lanes, 1) if lanes else value


def unpack(load, start, width, rows):
    lane = lane_index((rows, LANES))
    tile, shift = divmod(start, LANES)
    value = load(tile)
    if shift + width > LANES:
        value = jnp.where(lane >= shift, value, load(tile + 1))
    return jnp.where(lane < width, turn(value, -shift), 0.0)


def column_kernel(width, pitch, x_hbm, mask_hbm, table_hbm, out_ref, x, mask, table, left, x_sem, mask_sem, table_sem):
    channels, rows = x.shape[0], x.shape[1]
    chunks, parts = table.shape[0], out_ref.shape[0]
    x_copies = [pltpu.make_async_copy(x_hbm.at[0, c], x.at[c], x_sem.at[c]) for c in range(channels)]
    mask_copies = [pltpu.make_async_copy(mask_hbm.at[0, c], mask.at[c], mask_sem.at[c]) for c in range(channels)]
    table_copies = [pltpu.make_async_copy(table_hbm.at[n], table.at[n], table_sem.at[n]) for n in range(chunks)]
    for c in range(channels):
        mask_copies[c].start()
        x_copies[c].start()
    for copy in table_copies:
        copy.start()
    whole = rows // GROUP * GROUP
    tail = []
    for c in range(channels):
        mask_copies[c].wait()
        x_copies[c].wait()
        masked = x[c].astype(F32) * mask[c].astype(F32)
        left[c * whole : (c + 1) * whole] = masked[:whole].astype(BF16)
        tail.append(masked[whole:])
    spare = left.shape[0] - channels * rows
    if spare:
        tail.append(jnp.zeros((spare, left.shape[1]), F32))
    left[channels * whole :] = jnp.concatenate(tail, axis=0).astype(BF16)

    lane = lane_index((GROUP, LANES))
    for n in range(chunks):
        table_copies[n].wait()
        result = jnp.dot(left[...], table[n], preferred_element_type=F32)
        for k in range(parts // chunks):
            tile, shift = divmod(k * pitch, LANES)
            packed = Packed(out_ref.shape[2] // LANES)
            for g in range(left.shape[0] // GROUP):
                at = slice(g * GROUP, (g + 1) * GROUP)
                value = result[at, tile * LANES : (tile + 1) * LANES]
                if shift + width > LANES:
                    value = jnp.where(lane >= shift, value, result[at, (tile + 1) * LANES : (tile + 2) * LANES])
                packed.put(turn(value, g * width - shift), g * width, width)
            out_ref[n * (parts // chunks) + k] = jnp.concatenate(packed.tiles, axis=1).astype(BF16)


def split_rows(blocks, whole):
    groups = [v[a : a + GROUP] for v in blocks for a in range(0, whole, GROUP)]
    tail = [v[whole : whole + 8] for v in blocks]
    last = blocks[0][whole + 8 : whole + 16]
    for c in range(1, len(blocks)):
        last = last + pltpu.roll(blocks[c][whole + 8 : whole + 16], c, 0)
    tail.append(last)
    return groups + [jnp.concatenate(tail[i : i + 2], axis=0) for i in range(0, len(tail), 2)]


def join_rows(groups, channels, whole):
    per = whole // GROUP
    tail = []
    for value in groups[channels * per :]:
        tail += [value[:8], value[8:]]
    blocks = []
    for c in range(channels):
        last = pltpu.roll(tail[channels], 8 - c, 0) if c else tail[channels]
        blocks.append(jnp.concatenate(groups[c * per : (c + 1) * per] + [tail[c], last], axis=0))
    return blocks


def row_kernel(half, channels, rows_up, x_ref, table_ref, out_ref, right):
    width = 2 * half
    parts = x_ref.shape[0]
    depth = parts * GROUP
    steps = right.shape[0] // depth
    tiles = out_ref.shape[2] // LANES // 2

    def load(tile):
        return x_ref[:, :, tile * LANES : (tile + 1) * LANES].reshape(depth, LANES).astype(F32)

    row_in_group = lax.broadcasted_iota(jnp.int32, (depth, LANES), 0) % GROUP
    for c in range(channels):
        lanes = slice(c * LANES, (c + 1) * LANES)
        for a in range(steps - 1):
            value = unpack(load, (c * (steps - 1) + a) * width, width, depth)
            right[a * depth : (a + 1) * depth, lanes] = value.astype(BF16)
        value = unpack(load, (channels * (steps - 1) + c // 2) * width, width, depth)
        value = jnp.where((row_in_group >= GROUP // 2) == (c % 2 == 1), value, 0.0)
        right[(steps - 1) * depth :, lanes] = value.astype(BF16)

    for q in range(out_ref.shape[0] // 2):
        top = 2 * q * rows_up
        result = jnp.dot(table_ref[top : top + 2 * rows_up], right[...], preferred_element_type=F32)
        sides = []
        for at in (0, rows_up):
            blocks = [result[at : at + rows_up, c * LANES : (c + 1) * LANES] for c in range(channels)]
            sides.append(split_rows(blocks, rows_up - GROUP))
        out = [Packed(tiles) for _ in range(4)]
        for g, (even, odd) in enumerate(zip(*sides)):
            start = g * half
            real_even, real_odd = turn(even, start), turn(odd, start - half)
            imag_even, imag_odd = turn(even, start - half), turn(odd, start)
            out[0].put(real_even + real_odd, start, half)
            out[1].put(imag_even - imag_odd, start, half)
            out[2].put(real_even - real_odd, start, half)
            out[3].put(imag_even + imag_odd, start, half)
        for place, values in ((q, out[:2]), (out_ref.shape[0] - 1 - q, out[2:])):
            joined = jnp.concatenate(values[0].tiles + values[1].tiles, axis=1)
            out_ref[place] = joined.astype(BF16)


def lag_kernel(lag_ref, z_ref, out_ref, wide):
    slots, rows, lanes = z_ref.shape
    middle = lanes // 2
    for t in range(slots):
        wide[t] = z_ref[t].astype(F32)
    for entry in range(out_ref.shape[0]):
        lag = lag_ref[entry]

        def add(t, sums):
            early_real, early_imag = wide[t, :, :middle], wide[t, :, middle:]
            late_real, late_imag = wide[t + lag, :, :middle], wide[t + lag, :, middle:]
            return (
                sums[0] + (early_real * late_real + early_imag * late_imag),
                sums[1] + (early_imag * late_real - early_real * late_imag),
            )

        zero = jnp.zeros((rows, middle), F32)
        sums = lax.fori_loop(0, slots - lag, add, (zero, zero))
        scale = 1.0 / jnp.broadcast_to((slots - lag).astype(F32), (rows, LANES))
        for part in range(2):
            for at in range(0, middle, LANES):
                value = sums[part][:, at : at + LANES] * scale
                out_ref[entry, :, part * middle + at : part * middle + at + LANES] = value.astype(BF16)


def place_kernel(half, channels, rows_up, own_ref, other_ref, spread_ref, out_ref, both, spread):
    block = out_ref.shape[3]
    whole = rows_up - GROUP
    groups = channels * (rows_up // GROUP - 1) + (channels + 2) // 2
    middle = own_ref.shape[2] // 2
    at_row = lax.broadcasted_iota(jnp.int32, (rows_up, rows_up), 0)
    at_col = lax.broadcasted_iota(jnp.int32, (rows_up, rows_up), 1)
    back = lax.axis_index("slot") * 2 >= lax.axis_size("slot")
    source = jnp.where(back, block - at_row, at_row)
    order = (source == at_col).astype(F32).astype(BF16)
    entries = out_ref.shape[1]
    for part in range(2):
        for entry in range(entries):
            sides = []
            for ref in (own_ref, other_ref):

                def load(tile):
                    return ref[entry, :, tile * LANES : (tile + 1) * LANES].astype(F32)

                values = [unpack(load, part * middle + g * half, half, GROUP) for g in range(groups)]
                sides.append(join_rows(values, channels, whole))
            for c in range(channels):
                at = (part * entries + entry) * channels + c
                value = jnp.concatenate([sides[0][c], sides[1][c]], axis=1)
                both[at * rows_up : (at + 1) * rows_up] = value.astype(BF16)
    for part in range(2):
        for entry in range(entries):
            for c in range(channels):
                at = (part * entries + entry) * channels + c
                value = jnp.dot(both[at * rows_up : (at + 1) * rows_up], spread_ref[part], preferred_element_type=F32)
                spread[:, at * LANES : (at + 1) * LANES] = value.astype(BF16)
    for part in range(2):
        for entry in range(entries):
            for c in range(channels):
                at = (part * entries + entry) * channels + c
                value = jnp.dot(order, spread[:, at * LANES : (at + 1) * LANES], preferred_element_type=F32)
                out_ref[part, entry, c] = value[:block, :block]


def spread_table(block, half):
    table = np.zeros((2, 2 * LANES, LANES))
    for j in range(block):
        if j < half:
            table[:, j, j] = 1.0
        else:
            table[:, LANES + block - j, j] = (1.0, -1.0)
    return table.astype(ml_dtypes.bfloat16)


def up(value, unit):
    return -(-value // unit) * unit


def on_device(slots, parts, innovation, clear_mask, lag_list):
    _, channels, rows, cols = innovation.shape
    length = rows * parts
    block = cols // parts
    half = block // 2 + 1
    width = 2 * half
    entries = lag_list.shape[0]
    whole_vmem = pl.BlockSpec(memory_space=pltpu.VMEM)
    limit = pltpu.CompilerParams(vmem_limit_bytes=24 * 2**20)

    left_rows = up(channels * rows, GROUP)
    packed = up(left_rows // GROUP * width, LANES)
    pitch, chunks = 96, 2
    table = column_table(cols, parts, half, pitch, chunks)
    g = pl.pallas_call(
        functools.partial(column_kernel, width, pitch),
        in_specs=[pl.BlockSpec(memory_space=pl.ANY)] * 3,
        out_specs=whole_vmem,
        out_shape=jax.ShapeDtypeStruct((parts, GROUP, packed), BF16),
        scratch_shapes=[
            pltpu.VMEM(innovation.shape[1:], BF16),
            pltpu.VMEM(clear_mask.shape[1:], jnp.int32),
            pltpu.VMEM(table.shape, BF16),
            pltpu.VMEM((left_rows, cols), BF16),
            pltpu.SemaphoreType.DMA((channels,)),
            pltpu.SemaphoreType.DMA((channels,)),
            pltpu.SemaphoreType.DMA((chunks,)),
        ],
        compiler_params=pltpu.CompilerParams(vmem_limit_bytes=60 * 2**20),
        name="columns",
    )(innovation, clear_mask, jnp.asarray(table))
    g = lax.all_to_all(g, "row", 0, 0, tiled=True)

    whole = rows // GROUP
    order = [
        p * rows + (a * GROUP + b if a < whole else whole * GROUP + b % (GROUP // 2))
        for a in range(whole + 1)
        for p in range(parts)
        for b in range(GROUP)
    ]
    ky_block = length // slots
    rows_up = up(ky_block + 1, GROUP)
    table = row_table(length, slots, rows_up, np.array(order))
    packed = 2 * up((channels * (rows_up // GROUP - 1) + (channels + 2) // 2) * half, LANES)
    f = pl.pallas_call(
        functools.partial(row_kernel, half, channels, rows_up),
        in_specs=[whole_vmem] * 2,
        out_specs=whole_vmem,
        out_shape=jax.ShapeDtypeStruct((slots, GROUP, packed), BF16),
        scratch_shapes=[pltpu.VMEM((table.shape[1], channels * LANES), BF16)],
        compiler_params=limit,
        name="rows",
    )(g, jnp.asarray(table))
    f = lax.all_to_all(f, "slot", 0, 0, tiled=True)

    own = pl.pallas_call(
        lag_kernel,
        in_specs=[pl.BlockSpec(memory_space=pltpu.SMEM), whole_vmem],
        out_specs=whole_vmem,
        out_shape=jax.ShapeDtypeStruct((entries, GROUP, packed), BF16),
        scratch_shapes=[pltpu.VMEM((slots, GROUP, packed), F32)],
        compiler_params=limit,
        name="lags",
    )(lag_list, f)

    mirror = [
        (s * parts + p, (slots - 1 - s) * parts + parts - 1 - p) for s in range(slots) for p in range(parts)
    ]
    other = lax.ppermute(own, ("slot", "row"), mirror)

    planes = 2 * entries * channels
    return pl.pallas_call(
        functools.partial(place_kernel, half, channels, rows_up),
        in_specs=[whole_vmem] * 3,
        out_specs=whole_vmem,
        out_shape=jax.ShapeDtypeStruct((2, entries, channels, ky_block, block), F32),
        scratch_shapes=[pltpu.VMEM((planes * rows_up, 2 * LANES), BF16), pltpu.VMEM((rows_up, planes * LANES), BF16)],
        compiler_params=limit,
        name="place",
    )(own, other, jnp.asarray(spread_table(block, half)))


def solution(mesh):
    placed = (P("slot", None, "row", None), P("slot", None, "row", None), P())
    return jax.shard_map(
        functools.partial(on_device, mesh.shape["slot"], mesh.shape["row"]),
        mesh=mesh,
        in_specs=placed,
        out_specs=P(None, None, None, "slot", "row"),
        check_vma=False,
    )
```

```python
import functools
import math

import jax
import jax.numpy as jnp
import ml_dtypes
import numpy as np
from jax import lax
from jax.experimental import pallas as pl
from jax.experimental.pallas import tpu as pltpu
from jax.sharding import PartitionSpec as P

F32 = jnp.float32
BF16 = jnp.bfloat16
LANES = 128
GROUP = 16


def phase(numbers, length):
    return (numbers % length) * (2.0 * math.pi / length)


def column_table(length, parts, half, pitch, chunks):
    block = length // parts
    kx = (np.arange(parts)[:, None] * block + np.arange(half)[None, :]) % length
    angles = phase(np.arange(length)[:, None, None] * kx[None], length)
    table = np.zeros((length, parts, pitch))
    table[:, :, :half] = np.cos(angles)
    table[:, :, half : 2 * half] = -np.sin(angles)
    table = (table / math.sqrt(length)).reshape(length, chunks, parts // chunks * pitch)
    return np.ascontiguousarray(table.transpose(1, 0, 2)).astype(ml_dtypes.bfloat16)


def row_table(length, parts, rows_up, row_order):
    block = length // parts
    ky = np.arange(parts // 2)[:, None] * block + np.arange(block + 1)[None, :]
    angles = phase(ky[:, :, None] * row_order[None, None, :], length)
    table = np.zeros((parts // 2, 2, rows_up, row_order.size))
    table[:, 0, : block + 1] = np.cos(angles)
    table[:, 1, : block + 1] = np.sin(angles)
    return (table / math.sqrt(length)).reshape(-1, row_order.size).astype(ml_dtypes.bfloat16)


def lane_index(shape):
    return lax.broadcasted_iota(jnp.int32, shape, len(shape) - 1)


class Packed:
    def __init__(self, tiles):
        self.tiles = [jnp.zeros((GROUP, LANES), F32) for _ in range(tiles)]
        self.lane = lane_index((GROUP, LANES))

    def put(self, value, start, width):
        tile, shift = divmod(start, LANES)
        inside = self.lane >= shift
        if shift + width <= LANES:
            inside &= self.lane < shift + width
        else:
            after = self.lane < shift + width - LANES
            self.tiles[tile + 1] = jnp.where(after, value, self.tiles[tile + 1])
        self.tiles[tile] = jnp.where(inside, value, self.tiles[tile])


def turn(value, lanes):
    lanes %= LANES
    return pltpu.roll(value, lanes, 1) if lanes else value


def unpack(load, start, width, rows):
    lane = lane_index((rows, LANES))
    tile, shift = divmod(start, LANES)
    value = load(tile)
    if shift + width > LANES:
        value = jnp.where(lane >= shift, value, load(tile + 1))
    return jnp.where(lane < width, turn(value, -shift), jnp.zeros((), BF16))


def column_kernel(width, pitch, x_hbm, mask_hbm, table_hbm, out_ref, x, mask, table, left, x_sem, mask_sem, table_sem):
    channels, rows = x.shape[0], x.shape[1]
    chunks, parts = table.shape[0], out_ref.shape[0]
    x_copies = [pltpu.make_async_copy(x_hbm.at[0, c], x.at[c], x_sem.at[c]) for c in range(channels)]
    mask_copies = [pltpu.make_async_copy(mask_hbm.at[0, c], mask.at[c], mask_sem.at[c]) for c in range(channels)]
    table_copies = [pltpu.make_async_copy(table_hbm.at[n], table.at[n], table_sem.at[n]) for n in range(chunks)]
    for c in range(channels):
        mask_copies[c].start()
        x_copies[c].start()
    for copy in table_copies:
        copy.start()
    whole = rows // GROUP * GROUP
    tail = []
    for c in range(channels):
        mask_copies[c].wait()
        x_copies[c].wait()
        masked = x[c].astype(F32) * mask[c].astype(F32)
        left[c * whole : (c + 1) * whole] = masked[:whole].astype(BF16)
        tail.append(masked[whole:])
    spare = left.shape[0] - channels * rows
    if spare:
        tail.append(jnp.zeros((spare, left.shape[1]), F32))
    left[channels * whole :] = jnp.concatenate(tail, axis=0).astype(BF16)

    lane = lane_index((GROUP, LANES))
    for n in range(chunks):
        table_copies[n].wait()
        result = jnp.dot(left[...], table[n], preferred_element_type=F32)
        for k in range(parts // chunks):
            tile, shift = divmod(k * pitch, LANES)
            packed = Packed(out_ref.shape[2] // LANES)
            for g in range(left.shape[0] // GROUP):
                at = slice(g * GROUP, (g + 1) * GROUP)
                value = result[at, tile * LANES : (tile + 1) * LANES]
                if shift + width > LANES:
                    value = jnp.where(lane >= shift, value, result[at, (tile + 1) * LANES : (tile + 2) * LANES])
                packed.put(turn(value, g * width - shift), g * width, width)
            out_ref[n * (parts // chunks) + k] = jnp.concatenate(packed.tiles, axis=1).astype(BF16)


def split_rows(blocks, whole):
    groups = [v[a : a + GROUP] for v in blocks for a in range(0, whole, GROUP)]
    tail = [v[whole : whole + 8] for v in blocks]
    last = blocks[0][whole + 8 : whole + 16]
    for c in range(1, len(blocks)):
        last = last + pltpu.roll(blocks[c][whole + 8 : whole + 16], c, 0)
    tail.append(last)
    return groups + [jnp.concatenate(tail[i : i + 2], axis=0) for i in range(0, len(tail), 2)]


def join_rows(groups, channels, whole):
    per = whole // GROUP
    tail = []
    for value in groups[channels * per :]:
        tail += [value[:8], value[8:]]
    blocks = []
    for c in range(channels):
        last = pltpu.roll(tail[channels], 8 - c, 0) if c else tail[channels]
        blocks.append(jnp.concatenate(groups[c * per : (c + 1) * per] + [tail[c], last], axis=0))
    return blocks


def row_kernel(half, channels, rows_up, x_ref, table_ref, out_ref, right):
    width = 2 * half
    parts = x_ref.shape[0]
    depth = parts * GROUP
    steps = right.shape[0] // depth
    tiles = out_ref.shape[2] // LANES // 2

    def load(tile):
        return x_ref[:, :, tile * LANES : (tile + 1) * LANES].reshape(depth, LANES)

    row_in_group = lax.broadcasted_iota(jnp.int32, (depth, LANES), 0) % GROUP
    for c in range(channels):
        lanes = slice(c * LANES, (c + 1) * LANES)
        for a in range(steps - 1):
            value = unpack(load, (c * (steps - 1) + a) * width, width, depth)
            right[a * depth : (a + 1) * depth, lanes] = value
        value = unpack(load, (channels * (steps - 1) + c // 2) * width, width, depth)
        value = jnp.where((row_in_group >= GROUP // 2) == (c % 2 == 1), value, jnp.zeros((), BF16))
        right[(steps - 1) * depth :, lanes] = value

    for q in range(out_ref.shape[0] // 2):
        top = 2 * q * rows_up
        result = jnp.dot(table_ref[top : top + 2 * rows_up], right[...], preferred_element_type=F32)
        sides = []
        for at in (0, rows_up):
            blocks = [result[at : at + rows_up, c * LANES : (c + 1) * LANES] for c in range(channels)]
            sides.append(split_rows(blocks, rows_up - GROUP))
        out = [Packed(tiles) for _ in range(4)]
        for g, (even, odd) in enumerate(zip(*sides)):
            start = g * half
            real_even, real_odd = turn(even, start), turn(odd, start - half)
            imag_even, imag_odd = turn(even, start - half), turn(odd, start)
            out[0].put(real_even + real_odd, start, half)
            out[1].put(imag_even - imag_odd, start, half)
            out[2].put(real_even - real_odd, start, half)
            out[3].put(imag_even + imag_odd, start, half)
        for place, values in ((q, out[:2]), (out_ref.shape[0] - 1 - q, out[2:])):
            joined = jnp.concatenate(values[0].tiles + values[1].tiles, axis=1)
            out_ref[place] = joined.astype(BF16)


def lag_kernel(lag_ref, z_ref, out_ref, wide):
    slots, rows, lanes = z_ref.shape
    middle = lanes // 2
    for t in range(slots):
        wide[t] = z_ref[t].astype(F32)
    for entry in range(out_ref.shape[0]):
        lag = lag_ref[entry]

        def add(t, sums):
            early_real, early_imag = wide[t, :, :middle], wide[t, :, middle:]
            late_real, late_imag = wide[t + lag, :, :middle], wide[t + lag, :, middle:]
            return (
                sums[0] + (early_real * late_real + early_imag * late_imag),
                sums[1] + (early_imag * late_real - early_real * late_imag),
            )

        zero = jnp.zeros((rows, middle), F32)
        sums = lax.fori_loop(0, slots - lag, add, (zero, zero))
        scale = 1.0 / jnp.broadcast_to((slots - lag).astype(F32), (rows, LANES))
        for part in range(2):
            for at in range(0, middle, LANES):
                value = sums[part][:, at : at + LANES] * scale
                out_ref[entry, :, part * middle + at : part * middle + at + LANES] = value.astype(BF16)


def place_kernel(half, channels, rows_up, own_ref, other_ref, spread_ref, out_ref, both, spread):
    block = out_ref.shape[3]
    whole = rows_up - GROUP
    groups = channels * (rows_up // GROUP - 1) + (channels + 2) // 2
    middle = own_ref.shape[2] // 2
    at_row = lax.broadcasted_iota(jnp.int32, (rows_up, rows_up), 0)
    at_col = lax.broadcasted_iota(jnp.int32, (rows_up, rows_up), 1)
    back = lax.axis_index("slot") * 2 >= lax.axis_size("slot")
    source = jnp.where(back, block - at_row, at_row)
    order = (source == at_col).astype(F32).astype(BF16)
    entries = out_ref.shape[1]
    for part in range(2):
        for entry in range(entries):
            sides = []
            for ref in (own_ref, other_ref):

                def load(tile):
                    return ref[entry, :, tile * LANES : (tile + 1) * LANES]

                values = [unpack(load, part * middle + g * half, half, GROUP).astype(F32) for g in range(groups)]
                sides.append(join_rows(values, channels, whole))
            for c in range(channels):
                at = (part * entries + entry) * channels + c
                value = jnp.concatenate([sides[0][c], sides[1][c]], axis=1)
                both[at * rows_up : (at + 1) * rows_up] = value.astype(BF16)
    for part in range(2):
        for entry in range(entries):
            for c in range(channels):
                at = (part * entries + entry) * channels + c
                value = jnp.dot(both[at * rows_up : (at + 1) * rows_up], spread_ref[part], preferred_element_type=F32)
                spread[:, at * LANES : (at + 1) * LANES] = value.astype(BF16)
    for part in range(2):
        for entry in range(entries):
            for c in range(channels):
                at = (part * entries + entry) * channels + c
                value = jnp.dot(order, spread[:, at * LANES : (at + 1) * LANES], preferred_element_type=F32)
                out_ref[part, entry, c] = value[:block, :block]


def spread_table(block, half):
    table = np.zeros((2, 2 * LANES, LANES))
    for j in range(block):
        if j < half:
            table[:, j, j] = 1.0
        else:
            table[:, LANES + block - j, j] = (1.0, -1.0)
    return table.astype(ml_dtypes.bfloat16)


def up(value, unit):
    return -(-value // unit) * unit


def on_device(slots, parts, innovation, clear_mask, lag_list):
    _, channels, rows, cols = innovation.shape
    length = rows * parts
    block = cols // parts
    half = block // 2 + 1
    width = 2 * half
    entries = lag_list.shape[0]
    whole_vmem = pl.BlockSpec(memory_space=pltpu.VMEM)
    limit = pltpu.CompilerParams(vmem_limit_bytes=24 * 2**20)

    left_rows = up(channels * rows, GROUP)
    packed = up(left_rows // GROUP * width, LANES)
    pitch, chunks = 96, 2
    table = column_table(cols, parts, half, pitch, chunks)
    g = pl.pallas_call(
        functools.partial(column_kernel, width, pitch),
        in_specs=[pl.BlockSpec(memory_space=pl.ANY)] * 3,
        out_specs=whole_vmem,
        out_shape=jax.ShapeDtypeStruct((parts, GROUP, packed), BF16),
        scratch_shapes=[
            pltpu.VMEM(innovation.shape[1:], BF16),
            pltpu.VMEM(clear_mask.shape[1:], jnp.int32),
            pltpu.VMEM(table.shape, BF16),
            pltpu.VMEM((left_rows, cols), BF16),
            pltpu.SemaphoreType.DMA((channels,)),
            pltpu.SemaphoreType.DMA((channels,)),
            pltpu.SemaphoreType.DMA((chunks,)),
        ],
        compiler_params=pltpu.CompilerParams(vmem_limit_bytes=57 * 2**20),
        name="columns",
    )(innovation, clear_mask, jnp.asarray(table))
    g = lax.all_to_all(g, "row", 0, 0, tiled=True)

    whole = rows // GROUP
    order = [
        p * rows + (a * GROUP + b if a < whole else whole * GROUP + b % (GROUP // 2))
        for a in range(whole + 1)
        for p in range(parts)
        for b in range(GROUP)
    ]
    ky_block = length // slots
    rows_up = up(ky_block + 1, GROUP)
    table = row_table(length, slots, rows_up, np.array(order))
    packed = 2 * up((channels * (rows_up // GROUP - 1) + (channels + 2) // 2) * half, LANES)
    f = pl.pallas_call(
        functools.partial(row_kernel, half, channels, rows_up),
        in_specs=[whole_vmem] * 2,
        out_specs=whole_vmem,
        out_shape=jax.ShapeDtypeStruct((slots, GROUP, packed), BF16),
        scratch_shapes=[pltpu.VMEM((table.shape[1], channels * LANES), BF16)],
        compiler_params=limit,
        name="rows",
    )(g, jnp.asarray(table))
    f = lax.all_to_all(f, "slot", 0, 0, tiled=True)

    own = pl.pallas_call(
        lag_kernel,
        in_specs=[pl.BlockSpec(memory_space=pltpu.SMEM), whole_vmem],
        out_specs=whole_vmem,
        out_shape=jax.ShapeDtypeStruct((entries, GROUP, packed), BF16),
        scratch_shapes=[pltpu.VMEM((slots, GROUP, packed), F32)],
        compiler_params=limit,
        name="lags",
    )(lag_list, f)

    mirror = [
        (s * parts + p, (slots - 1 - s) * parts + parts - 1 - p) for s in range(slots) for p in range(parts)
    ]
    other = lax.ppermute(own, ("slot", "row"), mirror)

    planes = 2 * entries * channels
    return pl.pallas_call(
        functools.partial(place_kernel, half, channels, rows_up),
        in_specs=[whole_vmem] * 3,
        out_specs=whole_vmem,
        out_shape=jax.ShapeDtypeStruct((2, entries, channels, ky_block, block), F32),
        scratch_shapes=[pltpu.VMEM((planes * rows_up, 2 * LANES), BF16), pltpu.VMEM((rows_up, planes * LANES), BF16)],
        compiler_params=limit,
        name="place",
    )(own, other, jnp.asarray(spread_table(block, half)))


def solution(mesh):
    placed = (P("slot", None, "row", None), P("slot", None, "row", None), P())
    return jax.shard_map(
        functools.partial(on_device, mesh.shape["slot"], mesh.shape["row"]),
        mesh=mesh,
        in_specs=placed,
        out_specs=P(None, None, None, "slot", "row"),
        check_vma=False,
    )
```

```python
import functools
import math

import jax
import jax.numpy as jnp
import ml_dtypes
import numpy as np
from jax import lax
from jax.experimental import pallas as pl
from jax.experimental.pallas import tpu as pltpu
from jax.sharding import PartitionSpec as P

F32 = jnp.float32
BF16 = jnp.bfloat16
LANES = 128
GROUP = 16
CUT = 768


def phase(numbers, length):
    return (numbers % length) * (2.0 * math.pi / length)


def column_table(length, parts, half, pitch):
    block = length // parts
    kx = np.arange(parts // 2)[:, None] * block + np.arange(half)[None, :]
    angles = phase(np.arange(length)[:, None, None] * kx[None], length)
    table = np.zeros((length, parts // 2, pitch))
    table[:, :, :half] = np.cos(angles)
    table[:, :, half : 2 * half] = -np.sin(angles)
    return (table / math.sqrt(length)).reshape(length, parts // 2 * pitch).astype(ml_dtypes.bfloat16)


def row_table(length, parts, rows_up, row_order):
    block = length // parts
    ky = np.arange(parts // 4)[:, None] * block + np.arange(block + 1)[None, :]
    angles = phase(ky[:, :, None] * row_order[None, None, :], length)
    table = np.zeros((parts // 4, 2, rows_up, row_order.size))
    table[:, 0, : block + 1] = np.cos(angles)
    table[:, 1, : block + 1] = np.sin(angles)
    return (table / math.sqrt(length)).reshape(-1, row_order.size).astype(ml_dtypes.bfloat16)


def lane_index(shape):
    return lax.broadcasted_iota(jnp.int32, shape, len(shape) - 1)


class Packed:
    def __init__(self, tiles):
        self.tiles = [jnp.zeros((GROUP, LANES), F32) for _ in range(tiles)]
        self.lane = lane_index((GROUP, LANES))

    def put(self, value, start, width):
        tile, shift = divmod(start, LANES)
        inside = self.lane >= shift
        if shift + width <= LANES:
            inside &= self.lane < shift + width
        else:
            after = self.lane < shift + width - LANES
            self.tiles[tile + 1] = jnp.where(after, value, self.tiles[tile + 1])
        self.tiles[tile] = jnp.where(inside, value, self.tiles[tile])


def turn(value, lanes):
    lanes %= LANES
    return pltpu.roll(value, lanes, 1) if lanes else value


def unpack(load, start, width, rows):
    lane = lane_index((rows, LANES))
    tile, shift = divmod(start, LANES)
    value = load(tile)
    if shift + width > LANES:
        value = jnp.where(lane >= shift, value, load(tile + 1))
    return jnp.where(lane < width, turn(value, -shift), jnp.zeros((), BF16))


def column_kernel(
    width, pitch, x_hbm, mask_hbm, table_hbm, out_ref, x, mask, table, left, result, x_sem, mask_sem, table_sem
):
    channels, rows = x.shape[0], x.shape[1]
    parts, used = out_ref.shape[0], left.shape[0] // 2
    x_copies = [pltpu.make_async_copy(x_hbm.at[0, c], x.at[c], x_sem.at[c]) for c in range(channels)]
    mask_copies = [pltpu.make_async_copy(mask_hbm.at[0, c], mask.at[c], mask_sem.at[c]) for c in range(channels)]
    cuts = [slice(0, CUT), slice(CUT, table.shape[0])]
    table_copies = [pltpu.make_async_copy(table_hbm.at[k], table.at[k], table_sem.at[n]) for n, k in enumerate(cuts)]
    for c in range(channels):
        mask_copies[c].start()
        x_copies[c].start()
    for copy in table_copies:
        copy.start()
    whole = rows // GROUP * GROUP
    tail = []

    def store(at, value):
        odd = lane_index(value.shape) % 2 == 1
        left[at : at + value.shape[0]] = value.astype(BF16)
        left[used + at : used + at + value.shape[0]] = jnp.where(odd, -value, value).astype(BF16)

    for c in range(channels):
        mask_copies[c].wait()
        x_copies[c].wait()
        masked = x[c].astype(F32) * mask[c].astype(F32)
        store(c * whole, masked[:whole])
        tail.append(masked[whole:])
    spare = used - channels * rows
    if spare:
        tail.append(jnp.zeros((spare, left.shape[1]), F32))
    store(channels * whole, jnp.concatenate(tail, axis=0))

    for n, k in enumerate(cuts):
        table_copies[n].wait()
        value = jnp.dot(left[:, k], table[k], preferred_element_type=F32)
        result[...] = result[...] + value if n else value

    lane = lane_index((GROUP, LANES))
    for k in range(parts // 2):
        tile, shift = divmod(k * pitch, LANES)
        for side in range(2):
            packed = Packed(out_ref.shape[2] // LANES)
            for g in range(used // GROUP):
                at = slice(side * used + g * GROUP, side * used + (g + 1) * GROUP)
                value = result[at, tile * LANES : (tile + 1) * LANES]
                if shift + width > LANES:
                    value = jnp.where(lane >= shift, value, result[at, (tile + 1) * LANES : (tile + 2) * LANES])
                packed.put(turn(value, g * width - shift), g * width, width)
            out_ref[side * (parts // 2) + k] = jnp.concatenate(packed.tiles, axis=1).astype(BF16)


def split_rows(blocks, whole):
    groups = [v[a : a + GROUP] for v in blocks for a in range(0, whole, GROUP)]
    tail = [v[whole : whole + 8] for v in blocks]
    last = blocks[0][whole + 8 : whole + 16]
    for c in range(1, len(blocks)):
        last = last + pltpu.roll(blocks[c][whole + 8 : whole + 16], c, 0)
    tail.append(last)
    return groups + [jnp.concatenate(tail[i : i + 2], axis=0) for i in range(0, len(tail), 2)]


def join_rows(groups, channels, whole):
    per = whole // GROUP
    tail = []
    for value in groups[channels * per :]:
        tail += [value[:8], value[8:]]
    blocks = []
    for c in range(channels):
        last = pltpu.roll(tail[channels], 8 - c, 0) if c else tail[channels]
        blocks.append(jnp.concatenate(groups[c * per : (c + 1) * per] + [tail[c], last], axis=0))
    return blocks


def row_kernel(half, channels, rows_up, x_ref, table_ref, out_ref, right):
    width = 2 * half
    parts = x_ref.shape[0]
    depth = parts * GROUP
    steps = right.shape[0] // depth
    tiles = out_ref.shape[2] // LANES // 2

    def load(tile):
        return x_ref[:, :, tile * LANES : (tile + 1) * LANES].reshape(depth, LANES)

    row_in_group = lax.broadcasted_iota(jnp.int32, (depth, LANES), 0) % GROUP
    odd_row = row_in_group % 2 == 1

    def store(a, c, value):
        at = slice(a * depth, (a + 1) * depth)
        right[at, c * LANES : (c + 1) * LANES] = value
        right[at, (channels + c) * LANES : (channels + c + 1) * LANES] = jnp.where(odd_row, -value, value)

    for c in range(channels):
        for a in range(steps - 1):
            store(a, c, unpack(load, (c * (steps - 1) + a) * width, width, depth))
        value = unpack(load, (channels * (steps - 1) + c // 2) * width, width, depth)
        value = jnp.where((row_in_group >= GROUP // 2) == (c % 2 == 1), value, jnp.zeros((), BF16))
        store(steps - 1, c, value)

    slots = out_ref.shape[0]
    for q in range(slots // 4):
        top = 2 * q * rows_up
        result = jnp.dot(table_ref[top : top + 2 * rows_up], right[...], preferred_element_type=F32)
        for shifted in range(2):
            sides = []
            for at in (0, rows_up):
                lanes = [slice((shifted * channels + c) * LANES, (shifted * channels + c + 1) * LANES) for c in range(channels)]
                sides.append(split_rows([result[at : at + rows_up, l] for l in lanes], rows_up - GROUP))
            out = [Packed(tiles) for _ in range(4)]
            for g, (even, odd) in enumerate(zip(*sides)):
                start = g * half
                real_even, real_odd = turn(even, start), turn(odd, start - half)
                imag_even, imag_odd = turn(even, start - half), turn(odd, start)
                out[0].put(real_even + real_odd, start, half)
                out[1].put(imag_even - imag_odd, start, half)
                out[2].put(real_even - real_odd, start, half)
                out[3].put(imag_even + imag_odd, start, half)
            place = q + shifted * (slots // 2)
            for at, values in ((place, out[:2]), (slots - 1 - place, out[2:])):
                joined = jnp.concatenate(values[0].tiles + values[1].tiles, axis=1)
                out_ref[at] = joined.astype(BF16)


def zero_entry(lag_ref, entries):
    found = entries - 1
    for entry in reversed(range(entries - 1)):
        found = jnp.where(lag_ref[entry] == 0, entry, found)
    return found


def lag_kernel(lag_hbm, z_ref, own_ref, sent_ref, pick_ref, wide, lag_ref, lag_sem):
    slots, rows, lanes = z_ref.shape
    middle = lanes // 2
    entries = own_ref.shape[0] // 2
    lag_copy = pltpu.make_async_copy(lag_hbm, lag_ref, lag_sem)
    lag_copy.start()
    for t in range(slots):
        wide[t] = z_ref[t].astype(F32)
    lag_copy.wait()
    still = zero_entry(lag_ref, entries)
    for entry in range(entries):
        for earlier, here in enumerate((entry < still, entry > still)):
            pick_ref[entry, earlier] = jnp.broadcast_to(jnp.where(here, 1.0, 0.0), pick_ref.shape[2:]).astype(BF16)
    for entry in range(entries):
        lag = lag_ref[entry]

        def add(t, sums):
            early_real, early_imag = wide[t, :, :middle], wide[t, :, middle:]
            late_real, late_imag = wide[t + lag, :, :middle], wide[t + lag, :, middle:]
            return (
                sums[0] + (early_real * late_real + early_imag * late_imag),
                sums[1] + (early_imag * late_real - early_real * late_imag),
            )

        zero = jnp.zeros((rows, middle), F32)
        sums = lax.fori_loop(0, slots - lag, add, (zero, zero))
        scale = 1.0 / jnp.broadcast_to((slots - lag).astype(F32), (rows, LANES))
        place = entries + entry - jnp.where(entry > still, 1, 0)
        for at in range(0, middle, LANES):
            value = (sums[0][:, at : at + LANES] * scale).astype(BF16)
            own_ref[entry, :, at : at + LANES] = value
            sent_ref[entry, :, at : at + LANES] = value
            own_ref[entries + entry, :, at : at + LANES] = (sums[1][:, at : at + LANES] * scale).astype(BF16)

        @pl.when(entry != still)
        def _():
            sent_ref[place] = own_ref[entries + entry]


def place_kernel(half, channels, rows_up, own_ref, other_ref, pick_ref, spread_ref, out_ref, imag, both, spread):
    block = out_ref.shape[3]
    whole = rows_up - GROUP
    groups = channels * (rows_up // GROUP - 1) + (channels + 2) // 2
    at_row = lax.broadcasted_iota(jnp.int32, (rows_up, rows_up), 0)
    at_col = lax.broadcasted_iota(jnp.int32, (rows_up, rows_up), 1)
    back = lax.axis_index("slot") // (lax.axis_size("slot") // 4) % 2 == 1
    source = jnp.where(back, block - at_row, at_row)
    order = (source == at_col).astype(F32).astype(BF16)
    entries = out_ref.shape[1]
    for entry in range(entries):
        for at in range(0, imag.shape[2], LANES):
            value = jnp.zeros((GROUP, LANES), BF16)
            if entry < entries - 1:
                value += pick_ref[entry, 0] * other_ref[entries + entry, :, at : at + LANES]
            if entry > 0:
                value += pick_ref[entry, 1] * other_ref[entries + entry - 1, :, at : at + LANES]
            imag[entry, :, at : at + LANES] = value
    for part in range(2):
        for entry in range(entries):
            sides = []
            for mirrored in range(2):

                ref, first = ((own_ref, part * entries), (imag if part else other_ref, 0))[mirrored]

                def load(tile):
                    return ref[first + entry, :, tile * LANES : (tile + 1) * LANES]

                values = [unpack(load, g * half, half, GROUP).astype(F32) for g in range(groups)]
                sides.append(join_rows(values, channels, whole))
            for c in range(channels):
                at = (part * entries + entry) * channels + c
                value = jnp.concatenate([sides[0][c], sides[1][c]], axis=1)
                both[at * rows_up : (at + 1) * rows_up] = value.astype(BF16)
    for part in range(2):
        for entry in range(entries):
            for c in range(channels):
                at = (part * entries + entry) * channels + c
                value = jnp.dot(both[at * rows_up : (at + 1) * rows_up], spread_ref[part], preferred_element_type=F32)
                spread[:, at * LANES : (at + 1) * LANES] = value.astype(BF16)
    for part in range(2):
        for entry in range(entries):
            for c in range(channels):
                at = (part * entries + entry) * channels + c
                value = jnp.dot(order, spread[:, at * LANES : (at + 1) * LANES], preferred_element_type=F32)
                out_ref[part, entry, c] = value[:block, :block]


def spread_table(block, half):
    table = np.zeros((2, 2 * LANES, LANES))
    for j in range(block):
        if j < half:
            table[:, j, j] = 1.0
        else:
            table[:, LANES + block - j, j] = (1.0, -1.0)
    return table.astype(ml_dtypes.bfloat16)


def up(value, unit):
    return -(-value // unit) * unit


def on_device(slots, parts, innovation, clear_mask, lag_list):
    _, channels, rows, cols = innovation.shape
    length = rows * parts
    block = cols // parts
    half = block // 2 + 1
    width = 2 * half
    entries = lag_list.shape[0]
    whole_vmem = pl.BlockSpec(memory_space=pltpu.VMEM)
    limit = pltpu.CompilerParams(vmem_limit_bytes=24 * 2**20)

    left_rows = up(channels * rows, GROUP)
    packed = up(left_rows // GROUP * width, LANES)
    pitch = 96
    table = column_table(cols, parts, half, pitch)
    g = pl.pallas_call(
        functools.partial(column_kernel, width, pitch),
        in_specs=[pl.BlockSpec(memory_space=pl.ANY)] * 3,
        out_specs=whole_vmem,
        out_shape=jax.ShapeDtypeStruct((parts, GROUP, packed), BF16),
        scratch_shapes=[
            pltpu.VMEM(innovation.shape[1:], BF16),
            pltpu.VMEM(clear_mask.shape[1:], jnp.int32),
            pltpu.VMEM(table.shape, BF16),
            pltpu.VMEM((2 * left_rows, cols), BF16),
            pltpu.VMEM((2 * left_rows, parts // 2 * pitch), F32),
            pltpu.SemaphoreType.DMA((channels,)),
            pltpu.SemaphoreType.DMA((channels,)),
            pltpu.SemaphoreType.DMA((2,)),
        ],
        compiler_params=pltpu.CompilerParams(vmem_limit_bytes=57 * 2**20),
        name="columns",
    )(innovation, clear_mask, jnp.asarray(table))
    g = lax.all_to_all(g, "row", 0, 0, tiled=True)

    whole = rows // GROUP
    order = [
        p * rows + (a * GROUP + b if a < whole else whole * GROUP + b % (GROUP // 2))
        for a in range(whole + 1)
        for p in range(parts)
        for b in range(GROUP)
    ]
    ky_block = length // slots
    rows_up = up(ky_block + 1, GROUP)
    table = row_table(length, slots, rows_up, np.array(order))
    packed = 2 * up((channels * (rows_up // GROUP - 1) + (channels + 2) // 2) * half, LANES)
    f = pl.pallas_call(
        functools.partial(row_kernel, half, channels, rows_up),
        in_specs=[whole_vmem] * 2,
        out_specs=whole_vmem,
        out_shape=jax.ShapeDtypeStruct((slots, GROUP, packed), BF16),
        scratch_shapes=[pltpu.VMEM((table.shape[1], 2 * channels * LANES), BF16)],
        compiler_params=limit,
        name="rows",
    )(g, jnp.asarray(table))
    f = lax.all_to_all(f, "slot", 0, 0, tiled=True)

    own, sent, pick = pl.pallas_call(
        lag_kernel,
        in_specs=[pl.BlockSpec(memory_space=pl.ANY), whole_vmem],
        out_specs=[whole_vmem] * 3,
        out_shape=[
            jax.ShapeDtypeStruct((2 * entries, GROUP, packed // 2), BF16),
            jax.ShapeDtypeStruct((2 * entries - 1, GROUP, packed // 2), BF16),
            jax.ShapeDtypeStruct((entries, 2, GROUP, LANES), BF16),
        ],
        scratch_shapes=[
            pltpu.VMEM((slots, GROUP, packed), F32),
            pltpu.SMEM((entries,), jnp.int32),
            pltpu.SemaphoreType.DMA(()),
        ],
        compiler_params=limit,
        name="lags",
    )(lag_list, f)

    mirror = [
        (s * parts + p, (slots - 1 - s) * parts + parts - 1 - p) for s in range(slots) for p in range(parts)
    ]
    other = lax.ppermute(sent, ("slot", "row"), mirror)

    planes = 2 * entries * channels
    return pl.pallas_call(
        functools.partial(place_kernel, half, channels, rows_up),
        in_specs=[whole_vmem] * 4,
        out_specs=whole_vmem,
        out_shape=jax.ShapeDtypeStruct((2, entries, channels, ky_block, block), F32),
        scratch_shapes=[
            pltpu.VMEM((entries, GROUP, packed // 2), BF16),
            pltpu.VMEM((planes * rows_up, 2 * LANES), BF16), pltpu.VMEM((rows_up, planes * LANES), BF16)],
        compiler_params=limit,
        name="place",
    )(own, other, pick, jnp.asarray(spread_table(block, half)))


def solution(mesh):
    placed = (P("slot", None, "row", None), P("slot", None, "row", None), P())
    return jax.shard_map(
        functools.partial(on_device, mesh.shape["slot"], mesh.shape["row"]),
        mesh=mesh,
        in_specs=placed,
        out_specs=P(None, None, None, "slot", "row"),
        check_vma=False,
    )
```

```python
import functools
import math

import jax
import jax.numpy as jnp
import ml_dtypes
import numpy as np
from jax import lax
from jax.experimental import pallas as pl
from jax.experimental.pallas import tpu as pltpu
from jax.sharding import PartitionSpec as P

F32 = jnp.float32
BF16 = jnp.bfloat16
LANES = 128
GROUP = 16
CUT = 768


def phase(numbers, length):
    return (numbers % length) * (2.0 * math.pi / length)


def column_table(length, parts, half, pitch):
    block = length // parts
    kx = np.arange(parts // 2)[:, None] * block + np.arange(half)[None, :]
    angles = phase(np.arange(length)[:, None, None] * kx[None], length)
    table = np.zeros((length, parts // 2, pitch))
    table[:, :, :half] = np.cos(angles)
    table[:, :, half : 2 * half] = -np.sin(angles)
    return (table / math.sqrt(length)).reshape(length, parts // 2 * pitch).astype(ml_dtypes.bfloat16)


def row_table(length, parts, rows_up, row_order):
    block = length // parts
    ky = np.arange(parts // 4)[:, None] * block + np.arange(block + 1)[None, :]
    angles = phase(ky[:, :, None] * row_order[None, None, :], length)
    table = np.zeros((parts // 4, 2, rows_up, row_order.size))
    table[:, 0, : block + 1] = np.cos(angles)
    table[:, 1, : block + 1] = np.sin(angles)
    return (table / math.sqrt(length)).reshape(-1, row_order.size).astype(ml_dtypes.bfloat16)


def lane_index(shape):
    return lax.broadcasted_iota(jnp.int32, shape, len(shape) - 1)


class Packed:
    def __init__(self, tiles):
        self.tiles = [jnp.zeros((GROUP, LANES), F32) for _ in range(tiles)]
        self.lane = lane_index((GROUP, LANES))

    def put(self, value, start, width):
        tile, shift = divmod(start, LANES)
        inside = self.lane >= shift
        if shift + width <= LANES:
            inside &= self.lane < shift + width
        else:
            after = self.lane < shift + width - LANES
            self.tiles[tile + 1] = jnp.where(after, value, self.tiles[tile + 1])
        self.tiles[tile] = jnp.where(inside, value, self.tiles[tile])


def turn(value, lanes):
    lanes %= LANES
    return pltpu.roll(value, lanes, 1) if lanes else value


def unpack(load, start, width, rows):
    lane = lane_index((rows, LANES))
    tile, shift = divmod(start, LANES)
    value = load(tile)
    if shift + width > LANES:
        value = jnp.where(lane >= shift, value, load(tile + 1))
    return jnp.where(lane < width, turn(value, -shift), jnp.zeros((), BF16))


def column_kernel(
    width, pitch, x_hbm, mask_hbm, table_hbm, out_ref, x, mask, table, left, result, x_sem, mask_sem, table_sem
):
    channels, rows = x.shape[0], x.shape[1]
    parts, used = out_ref.shape[0], left.shape[0] // 2
    x_copies = [pltpu.make_async_copy(x_hbm.at[0, c], x.at[c], x_sem.at[c]) for c in range(channels)]
    mask_copies = [pltpu.make_async_copy(mask_hbm.at[0, c], mask.at[c], mask_sem.at[c]) for c in range(channels)]
    cuts = [slice(0, CUT), slice(CUT, table.shape[0])]
    table_copies = [pltpu.make_async_copy(table_hbm.at[k], table.at[k], table_sem.at[n]) for n, k in enumerate(cuts)]
    for c in range(channels):
        mask_copies[c].start()
        x_copies[c].start()
    for copy in table_copies:
        copy.start()
    whole = rows // GROUP * GROUP
    tail = []

    def store(at, value):
        odd = lane_index(value.shape) % 2 == 1
        left[at : at + value.shape[0]] = value.astype(BF16)
        left[used + at : used + at + value.shape[0]] = jnp.where(odd, -value, value).astype(BF16)

    for c in range(channels):
        mask_copies[c].wait()
        x_copies[c].wait()
        masked = x[c].astype(F32) * mask[c].astype(F32)
        store(c * whole, masked[:whole])
        tail.append(masked[whole:])
    spare = used - channels * rows
    if spare:
        tail.append(jnp.zeros((spare, left.shape[1]), F32))
    store(channels * whole, jnp.concatenate(tail, axis=0))

    for n, k in enumerate(cuts):
        table_copies[n].wait()
        value = jnp.dot(left[:, k], table[k], preferred_element_type=F32)
        result[...] = result[...] + value if n else value

    lane = lane_index((GROUP, LANES))
    for k in range(parts // 2):
        tile, shift = divmod(k * pitch, LANES)
        for side in range(2):
            packed = Packed(out_ref.shape[2] // LANES)
            for g in range(used // GROUP):
                at = slice(side * used + g * GROUP, side * used + (g + 1) * GROUP)
                value = result[at, tile * LANES : (tile + 1) * LANES]
                if shift + width > LANES:
                    value = jnp.where(lane >= shift, value, result[at, (tile + 1) * LANES : (tile + 2) * LANES])
                packed.put(turn(value, g * width - shift), g * width, width)
            out_ref[side * (parts // 2) + k] = jnp.concatenate(packed.tiles, axis=1).astype(BF16)


def split_rows(blocks, whole):
    groups = [v[a : a + GROUP] for v in blocks for a in range(0, whole, GROUP)]
    tail = [v[whole : whole + 8] for v in blocks]
    last = blocks[0][whole + 8 : whole + 16]
    for c in range(1, len(blocks)):
        last = last + pltpu.roll(blocks[c][whole + 8 : whole + 16], c, 0)
    tail.append(last)
    return groups + [jnp.concatenate(tail[i : i + 2], axis=0) for i in range(0, len(tail), 2)]


def join_rows(groups, channels, whole):
    per = whole // GROUP
    tail = []
    for value in groups[channels * per :]:
        tail += [value[:8], value[8:]]
    blocks = []
    for c in range(channels):
        last = pltpu.roll(tail[channels], 8 - c, 0) if c else tail[channels]
        blocks.append(jnp.concatenate(groups[c * per : (c + 1) * per] + [tail[c], last], axis=0))
    return blocks


def row_kernel(half, channels, rows_up, x_ref, table_ref, out_ref, right):
    width = 2 * half
    parts = x_ref.shape[0]
    depth = parts * GROUP
    steps = right.shape[0] // depth
    tiles = out_ref.shape[2] // LANES // 2

    def load(tile):
        return x_ref[:, :, tile * LANES : (tile + 1) * LANES].reshape(depth, LANES)

    row_in_group = lax.broadcasted_iota(jnp.int32, (depth, LANES), 0) % GROUP
    odd_row = row_in_group % 2 == 1

    def store(a, c, value):
        at = slice(a * depth, (a + 1) * depth)
        right[at, c * LANES : (c + 1) * LANES] = value
        right[at, (channels + c) * LANES : (channels + c + 1) * LANES] = jnp.where(odd_row, -value, value)

    for c in range(channels):
        for a in range(steps - 1):
            store(a, c, unpack(load, (c * (steps - 1) + a) * width, width, depth))
        value = unpack(load, (channels * (steps - 1) + c // 2) * width, width, depth)
        value = jnp.where((row_in_group >= GROUP // 2) == (c % 2 == 1), value, jnp.zeros((), BF16))
        store(steps - 1, c, value)

    slots = out_ref.shape[0]
    for q in range(slots // 4):
        top = 2 * q * rows_up
        result = jnp.dot(table_ref[top : top + 2 * rows_up], right[...], preferred_element_type=F32)
        for shifted in range(2):
            sides = []
            for at in (0, rows_up):
                lanes = [slice((shifted * channels + c) * LANES, (shifted * channels + c + 1) * LANES) for c in range(channels)]
                sides.append(split_rows([result[at : at + rows_up, l] for l in lanes], rows_up - GROUP))
            out = [Packed(tiles) for _ in range(4)]
            for g, (even, odd) in enumerate(zip(*sides)):
                start = g * half
                real_even, real_odd = turn(even, start), turn(odd, start - half)
                imag_even, imag_odd = turn(even, start - half), turn(odd, start)
                out[0].put(real_even + real_odd, start, half)
                out[1].put(imag_even - imag_odd, start, half)
                out[2].put(real_even - real_odd, start, half)
                out[3].put(imag_even + imag_odd, start, half)
            place = q + shifted * (slots // 2)
            for at, values in ((place, out[:2]), (slots - 1 - place, out[2:])):
                joined = jnp.concatenate(values[0].tiles + values[1].tiles, axis=1)
                out_ref[at] = joined.astype(BF16)


def zero_entry(lag_ref, entries):
    found = entries - 1
    for entry in reversed(range(entries - 1)):
        found = jnp.where(lag_ref[entry] == 0, entry, found)
    return found


def lag_kernel(lag_hbm, z_ref, own_ref, sent_ref, pick_ref, wide, lag_ref, lag_sem):
    slots, rows, lanes = z_ref.shape
    middle = lanes // 2
    entries = own_ref.shape[0] // 2
    lag_copy = pltpu.make_async_copy(lag_hbm, lag_ref, lag_sem)
    lag_copy.start()
    for t in range(slots):
        wide[t] = z_ref[t].astype(F32)
    lag_copy.wait()
    still = zero_entry(lag_ref, entries)
    for entry in range(entries):
        for earlier, here in enumerate((entry < still, entry > still)):
            pick_ref[entry, earlier] = jnp.broadcast_to(jnp.where(here, 1.0, 0.0), pick_ref.shape[2:]).astype(BF16)
    for entry in range(entries):
        lag = lag_ref[entry]

        def add(t, sums):
            early_real, early_imag = wide[t, :, :middle], wide[t, :, middle:]
            late_real, late_imag = wide[t + lag, :, :middle], wide[t + lag, :, middle:]
            return (
                sums[0] + (early_real * late_real + early_imag * late_imag),
                sums[1] + (early_imag * late_real - early_real * late_imag),
            )

        zero = jnp.zeros((rows, middle), F32)
        count = slots - lag
        sums = lax.fori_loop(0, count // 2, lambda i, sums: add(2 * i + 1, add(2 * i, sums)), (zero, zero))
        sums = lax.fori_loop(count // 2 * 2, count, add, sums)
        scale = 1.0 / jnp.broadcast_to((slots - lag).astype(F32), (rows, LANES))
        place = entries + entry - jnp.where(entry > still, 1, 0)
        for at in range(0, middle, LANES):
            value = (sums[0][:, at : at + LANES] * scale).astype(BF16)
            own_ref[entry, :, at : at + LANES] = value
            sent_ref[entry, :, at : at + LANES] = value
            own_ref[entries + entry, :, at : at + LANES] = (sums[1][:, at : at + LANES] * scale).astype(BF16)

        @pl.when(entry != still)
        def _():
            sent_ref[place] = own_ref[entries + entry]


def place_kernel(half, channels, rows_up, own_ref, other_ref, pick_ref, spread_ref, out_hbm, out_ref, imag, both, spread, out_sem):
    block = out_ref.shape[3]
    whole = rows_up - GROUP
    groups = channels * (rows_up // GROUP - 1) + (channels + 2) // 2
    at_row = lax.broadcasted_iota(jnp.int32, (rows_up, rows_up), 0)
    at_col = lax.broadcasted_iota(jnp.int32, (rows_up, rows_up), 1)
    back = lax.axis_index("slot") // (lax.axis_size("slot") // 4) % 2 == 1
    source = jnp.where(back, block - at_row, at_row)
    order = (source == at_col).astype(F32).astype(BF16)
    entries = out_ref.shape[1]
    for entry in range(entries):
        for at in range(0, imag.shape[2], LANES):
            value = jnp.zeros((GROUP, LANES), BF16)
            if entry < entries - 1:
                value += pick_ref[entry, 0] * other_ref[entries + entry, :, at : at + LANES]
            if entry > 0:
                value += pick_ref[entry, 1] * other_ref[entries + entry - 1, :, at : at + LANES]
            imag[entry, :, at : at + LANES] = value
    for part in range(2):
        for entry in range(entries):
            sides = []
            for mirrored in range(2):

                ref, first = ((own_ref, part * entries), (imag if part else other_ref, 0))[mirrored]

                def load(tile):
                    return ref[first + entry, :, tile * LANES : (tile + 1) * LANES]

                values = [unpack(load, g * half, half, GROUP).astype(F32) for g in range(groups)]
                sides.append(join_rows(values, channels, whole))
            for c in range(channels):
                at = (part * entries + entry) * channels + c
                value = jnp.concatenate([sides[0][c], sides[1][c]], axis=1)
                both[at * rows_up : (at + 1) * rows_up] = value.astype(BF16)
    for part in range(2):
        for entry in range(entries):
            for c in range(channels):
                at = (part * entries + entry) * channels + c
                value = jnp.dot(both[at * rows_up : (at + 1) * rows_up], spread_ref[part], preferred_element_type=F32)
                spread[:, at * LANES : (at + 1) * LANES] = value.astype(BF16)
    copies = []
    for part in range(2):
        for entry in range(entries):
            for c in range(channels):
                at = (part * entries + entry) * channels + c
                value = jnp.dot(order, spread[:, at * LANES : (at + 1) * LANES], preferred_element_type=F32)
                out_ref[part, entry, c] = value[:block, :block]
            copies.append(
                pltpu.make_async_copy(
                    out_ref.at[part, entry], out_hbm.at[part, entry], out_sem.at[part * entries + entry]
                )
            )
            copies[-1].start()
    for copy in copies:
        copy.wait()


def spread_table(block, half):
    table = np.zeros((2, 2 * LANES, LANES))
    for j in range(block):
        if j < half:
            table[:, j, j] = 1.0
        else:
            table[:, LANES + block - j, j] = (1.0, -1.0)
    return table.astype(ml_dtypes.bfloat16)


def up(value, unit):
    return -(-value // unit) * unit


def on_device(slots, parts, innovation, clear_mask, lag_list):
    _, channels, rows, cols = innovation.shape
    length = rows * parts
    block = cols // parts
    half = block // 2 + 1
    width = 2 * half
    entries = lag_list.shape[0]
    whole_vmem = pl.BlockSpec(memory_space=pltpu.VMEM)
    limit = pltpu.CompilerParams(vmem_limit_bytes=24 * 2**20)

    left_rows = up(channels * rows, GROUP)
    packed = up(left_rows // GROUP * width, LANES)
    pitch = 96
    table = column_table(cols, parts, half, pitch)
    g = pl.pallas_call(
        functools.partial(column_kernel, width, pitch),
        in_specs=[pl.BlockSpec(memory_space=pl.ANY)] * 3,
        out_specs=whole_vmem,
        out_shape=pltpu.VMEM((parts, GROUP, packed), BF16),
        scratch_shapes=[
            pltpu.VMEM(innovation.shape[1:], BF16),
            pltpu.VMEM(clear_mask.shape[1:], jnp.int32),
            pltpu.VMEM(table.shape, BF16),
            pltpu.VMEM((2 * left_rows, cols), BF16),
            pltpu.VMEM((2 * left_rows, parts // 2 * pitch), F32),
            pltpu.SemaphoreType.DMA((channels,)),
            pltpu.SemaphoreType.DMA((channels,)),
            pltpu.SemaphoreType.DMA((2,)),
        ],
        compiler_params=pltpu.CompilerParams(vmem_limit_bytes=55 * 2**20),
        name="columns",
    )(innovation, clear_mask, jnp.asarray(table))
    g = lax.all_to_all(g, "row", 0, 0, tiled=True)

    whole = rows // GROUP
    order = [
        p * rows + (a * GROUP + b if a < whole else whole * GROUP + b % (GROUP // 2))
        for a in range(whole + 1)
        for p in range(parts)
        for b in range(GROUP)
    ]
    ky_block = length // slots
    rows_up = up(ky_block + 1, GROUP)
    table = row_table(length, slots, rows_up, np.array(order))
    packed = 2 * up((channels * (rows_up // GROUP - 1) + (channels + 2) // 2) * half, LANES)
    f = pl.pallas_call(
        functools.partial(row_kernel, half, channels, rows_up),
        in_specs=[whole_vmem] * 2,
        out_specs=whole_vmem,
        out_shape=jax.ShapeDtypeStruct((slots, GROUP, packed), BF16),
        scratch_shapes=[pltpu.VMEM((table.shape[1], 2 * channels * LANES), BF16)],
        compiler_params=limit,
        name="rows",
    )(g, jnp.asarray(table))
    f = lax.all_to_all(f, "slot", 0, 0, tiled=True)

    own, sent, pick = pl.pallas_call(
        lag_kernel,
        in_specs=[pl.BlockSpec(memory_space=pl.ANY), whole_vmem],
        out_specs=[whole_vmem] * 3,
        out_shape=[
            jax.ShapeDtypeStruct((2 * entries, GROUP, packed // 2), BF16),
            jax.ShapeDtypeStruct((2 * entries - 1, GROUP, packed // 2), BF16),
            jax.ShapeDtypeStruct((entries, 2, GROUP, LANES), BF16),
        ],
        scratch_shapes=[
            pltpu.VMEM((slots, GROUP, packed), F32),
            pltpu.SMEM((entries,), jnp.int32),
            pltpu.SemaphoreType.DMA(()),
        ],
        compiler_params=limit,
        name="lags",
    )(lag_list, f)

    mirror = [
        (s * parts + p, (slots - 1 - s) * parts + parts - 1 - p) for s in range(slots) for p in range(parts)
    ]
    other = lax.ppermute(sent, ("slot", "row"), mirror)

    planes = 2 * entries * channels
    return pl.pallas_call(
        functools.partial(place_kernel, half, channels, rows_up),
        in_specs=[whole_vmem] * 4,
        out_specs=pl.BlockSpec(memory_space=pl.ANY),
        out_shape=jax.ShapeDtypeStruct((2, entries, channels, ky_block, block), F32),
        scratch_shapes=[
            pltpu.VMEM((2, entries, channels, ky_block, block), F32),
            pltpu.VMEM((entries, GROUP, packed // 2), BF16),
            pltpu.VMEM((planes * rows_up, 2 * LANES), BF16),
            pltpu.VMEM((rows_up, planes * LANES), BF16),
            pltpu.SemaphoreType.DMA((2 * entries,)),
        ],
        compiler_params=limit,
        name="place",
    )(own, other, pick, jnp.asarray(spread_table(block, half)))


def solution(mesh):
    placed = (P("slot", None, "row", None), P("slot", None, "row", None), P())
    return jax.shard_map(
        functools.partial(on_device, mesh.shape["slot"], mesh.shape["row"]),
        mesh=mesh,
        in_specs=placed,
        out_specs=P(None, None, None, "slot", "row"),
        check_vma=False,
    )
```

```python
import functools
import math

import jax
import jax.numpy as jnp
import ml_dtypes
import numpy as np
from jax import lax
from jax.experimental import pallas as pl
from jax.experimental.pallas import tpu as pltpu
from jax.sharding import PartitionSpec as P

F32 = jnp.float32
BF16 = jnp.bfloat16
LANES = 128
GROUP = 16


def phase(numbers, length):
    return (numbers % length) * (2.0 * math.pi / length)


def column_table(length, parts, half, pitch):
    block = length // parts
    kx = np.arange(parts // 2)[:, None] * block + np.arange(half)[None, :]
    angles = phase(np.arange(length)[:, None, None] * kx[None], length)
    table = np.zeros((length, parts // 2, pitch))
    table[:, :, :half] = np.cos(angles)
    table[:, :, half : 2 * half] = -np.sin(angles)
    return (table / math.sqrt(length)).reshape(length, parts // 2 * pitch).astype(ml_dtypes.bfloat16)


def row_table(length, parts, rows_up, row_order):
    block = length // parts
    ky = np.arange(parts // 4)[:, None] * block + np.arange(block + 1)[None, :]
    angles = phase(ky[:, :, None] * row_order[None, None, :], length)
    table = np.zeros((parts // 4, 2, rows_up, row_order.size))
    table[:, 0, : block + 1] = np.cos(angles)
    table[:, 1, : block + 1] = np.sin(angles)
    return (table / math.sqrt(length)).reshape(-1, row_order.size).astype(ml_dtypes.bfloat16)


def lane_index(shape):
    return lax.broadcasted_iota(jnp.int32, shape, len(shape) - 1)


class Packed:
    def __init__(self, tiles):
        self.tiles = [jnp.zeros((GROUP, LANES), F32) for _ in range(tiles)]
        self.lane = lane_index((GROUP, LANES))

    def put(self, value, start, width):
        tile, shift = divmod(start, LANES)
        inside = self.lane >= shift
        if shift + width <= LANES:
            inside &= self.lane < shift + width
        else:
            after = self.lane < shift + width - LANES
            self.tiles[tile + 1] = jnp.where(after, value, self.tiles[tile + 1])
        self.tiles[tile] = jnp.where(inside, value, self.tiles[tile])


def turn(value, lanes):
    lanes %= LANES
    return pltpu.roll(value, lanes, 1) if lanes else value


def unpack(load, start, width, rows):
    lane = lane_index((rows, LANES))
    tile, shift = divmod(start, LANES)
    value = load(tile)
    if shift + width > LANES:
        value = jnp.where(lane >= shift, value, load(tile + 1))
    return jnp.where(lane < width, turn(value, -shift), jnp.zeros((), BF16))


def column_kernel(
    width,
    pitch,
    x_hbm,
    mask_hbm,
    table_hbm,
    next_hbm,
    out_ref,
    next_ref,
    x,
    mask,
    table,
    wide,
    left,
    result,
    x_sem,
    mask_sem,
    table_sem,
    next_sem,
):
    channels, rows = x.shape[0], x.shape[1]
    parts, used = out_ref.shape[0], left.shape[0] // 2
    x_copies = [pltpu.make_async_copy(x_hbm.at[0, c], x.at[c], x_sem.at[c]) for c in range(channels)]
    mask_copies = [pltpu.make_async_copy(mask_hbm.at[0, c], mask.at[c], mask_sem.at[c]) for c in range(channels)]
    table_copy = pltpu.make_async_copy(table_hbm, table, table_sem)
    for c in range(channels):
        mask_copies[c].start()
        x_copies[c].start()
    table_copy.start()
    next_copy = pltpu.make_async_copy(next_hbm, next_ref, next_sem)
    next_copy.start()
    groups, eight = rows // GROUP, GROUP // 2
    tail = []

    def store(group, pieces):
        value = jnp.concatenate(pieces, axis=0)
        odd = lane_index(value.shape) % 2 == 1
        at = group * GROUP
        left[at : at + GROUP] = value.astype(BF16)
        left[used + at : used + at + GROUP] = jnp.where(odd, -value, value).astype(BF16)

    for c in range(channels):
        mask_copies[c].wait()
        x_copies[c].wait()
        for tile in range(wide.shape[1]):
            lanes = slice(tile * LANES, (tile + 1) * LANES)
            wide[c, tile] = x[c, :, lanes].astype(F32) * mask[c, :, lanes].astype(F32)

        def every_other(first, count):
            return jnp.concatenate([wide[c, tile, pl.ds(first, count, 2)] for tile in range(wide.shape[1])], axis=1)

        for a in range(groups):
            store(c * groups + a, [every_other(a * GROUP + parity, eight) for parity in range(2)])
        tail.append([every_other(groups * GROUP + parity, eight // 2) for parity in range(2)])
    if channels % 2:
        tail.append([jnp.zeros((eight // 2, left.shape[1]), F32)] * 2)
    for i in range(0, len(tail), 2):
        store(channels * groups + i // 2, [tail[i + side][parity] for parity in range(2) for side in range(2)])

    table_copy.wait()
    result[...] = jnp.dot(left[...], table[...], preferred_element_type=F32)

    lane = lane_index((GROUP, LANES))
    for k in range(parts // 2):
        tile, shift = divmod(k * pitch, LANES)
        for side in range(2):
            packed = Packed(out_ref.shape[2] // LANES)
            for g in range(used // GROUP):
                at = slice(side * used + g * GROUP, side * used + (g + 1) * GROUP)
                value = result[at, tile * LANES : (tile + 1) * LANES]
                if shift + width > LANES:
                    value = jnp.where(lane >= shift, value, result[at, (tile + 1) * LANES : (tile + 2) * LANES])
                packed.put(turn(value, g * width - shift), g * width, width)
            out_ref[side * (parts // 2) + k] = jnp.concatenate(packed.tiles, axis=1).astype(BF16)
    next_copy.wait()


def split_rows(blocks, whole):
    groups = [v[a : a + GROUP] for v in blocks for a in range(0, whole, GROUP)]
    tail = [v[whole : whole + 8] for v in blocks]
    last = blocks[0][whole + 8 : whole + 16]
    for c in range(1, len(blocks)):
        last = last + pltpu.roll(blocks[c][whole + 8 : whole + 16], c, 0)
    tail.append(last)
    return groups + [jnp.concatenate(tail[i : i + 2], axis=0) for i in range(0, len(tail), 2)]


def join_rows(groups, channels, whole):
    per = whole // GROUP
    tail = []
    for value in groups[channels * per :]:
        tail += [value[:8], value[8:]]
    blocks = []
    for c in range(channels):
        last = pltpu.roll(tail[channels], 8 - c, 0) if c else tail[channels]
        blocks.append(jnp.concatenate(groups[c * per : (c + 1) * per] + [tail[c], last], axis=0))
    return blocks


def row_kernel(half, channels, rows_up, x_ref, table_ref, out_ref, right):
    width = 2 * half
    parts = x_ref.shape[0]
    depth = parts * GROUP
    eight = depth // 2
    steps = right.shape[1] // eight
    tiles = out_ref.shape[2] // LANES // 2

    def load(tile):
        return x_ref[:, :, tile * LANES : (tile + 1) * LANES].reshape(depth, LANES)

    row_in_half = lax.broadcasted_iota(jnp.int32, (eight, LANES), 0) % (GROUP // 2)

    for c in range(channels):
        for a in range(steps):
            last = a == steps - 1
            group = channels * (steps - 1) + c // 2 if last else c * (steps - 1) + a
            value = unpack(load, group * width, width, depth).astype(F32)
            value = value.reshape(parts, 2, GROUP // 2, LANES)
            for parity in range(2):
                half_rows = value[:, parity].reshape(eight, LANES)
                if last:
                    half_rows = jnp.where((row_in_half >= GROUP // 4) == (c % 2 == 1), half_rows, 0.0)
                right[parity, a * eight : (a + 1) * eight, c * LANES : (c + 1) * LANES] = half_rows.astype(BF16)

    slots, depth_all = out_ref.shape[0], right.shape[1]
    for q in range(slots // 4):
        rows_here = slice(2 * q * rows_up, 2 * (q + 1) * rows_up)
        sums = [
            jnp.dot(
                table_ref[rows_here, parity * depth_all : (parity + 1) * depth_all],
                right[parity],
                preferred_element_type=F32,
            )
            for parity in range(2)
        ]
        for shifted in range(2):
            result = sums[0] - sums[1] if shifted else sums[0] + sums[1]
            sides = []
            for at in (0, rows_up):
                lanes = [slice(c * LANES, (c + 1) * LANES) for c in range(channels)]
                sides.append(split_rows([result[at : at + rows_up, l] for l in lanes], rows_up - GROUP))
            out = [Packed(tiles) for _ in range(4)]
            for g, (even, odd) in enumerate(zip(*sides)):
                start = g * half
                real_even, real_odd = turn(even, start), turn(odd, start - half)
                imag_even, imag_odd = turn(even, start - half), turn(odd, start)
                out[0].put(real_even + real_odd, start, half)
                out[1].put(imag_even - imag_odd, start, half)
                out[2].put(real_even - real_odd, start, half)
                out[3].put(imag_even + imag_odd, start, half)
            place = q + shifted * (slots // 2)
            for at, values in ((place, out[:2]), (slots - 1 - place, out[2:])):
                joined = jnp.concatenate(values[0].tiles + values[1].tiles, axis=1)
                out_ref[at] = joined.astype(BF16)


def zero_entry(lag_ref, entries):
    found = entries - 1
    for entry in reversed(range(entries - 1)):
        found = jnp.where(lag_ref[entry] == 0, entry, found)
    return found


def lag_kernel(lag_hbm, z_ref, own_ref, sent_ref, pick_ref, wide, lag_ref, lag_sem):
    slots, rows, lanes = z_ref.shape
    middle = lanes // 2
    entries = own_ref.shape[0] // 2
    lag_copy = pltpu.make_async_copy(lag_hbm, lag_ref, lag_sem)
    lag_copy.start()
    for t in range(slots):
        wide[t] = z_ref[t].astype(F32)
    lag_copy.wait()
    still = zero_entry(lag_ref, entries)
    for entry in range(entries):
        for earlier, here in enumerate((entry < still, entry > still)):
            pick_ref[entry, earlier] = jnp.broadcast_to(jnp.where(here, 1.0, 0.0), pick_ref.shape[2:]).astype(BF16)
    for entry in range(entries):
        lag = lag_ref[entry]

        def add(t, sums):
            early_real, early_imag = wide[t, :, :middle], wide[t, :, middle:]
            late_real, late_imag = wide[t + lag, :, :middle], wide[t + lag, :, middle:]
            return (
                sums[0] + (early_real * late_real + early_imag * late_imag),
                sums[1] + (early_imag * late_real - early_real * late_imag),
            )

        zero = jnp.zeros((rows, middle), F32)
        count = slots - lag
        sums = lax.fori_loop(0, count // 2, lambda i, sums: add(2 * i + 1, add(2 * i, sums)), (zero, zero))
        sums = lax.fori_loop(count // 2 * 2, count, add, sums)
        scale = 1.0 / jnp.broadcast_to((slots - lag).astype(F32), (rows, LANES))
        place = entries + entry - jnp.where(entry > still, 1, 0)
        for at in range(0, middle, LANES):
            value = (sums[0][:, at : at + LANES] * scale).astype(BF16)
            own_ref[entry, :, at : at + LANES] = value
            sent_ref[entry, :, at : at + LANES] = value
            own_ref[entries + entry, :, at : at + LANES] = (sums[1][:, at : at + LANES] * scale).astype(BF16)

        @pl.when(entry != still)
        def _():
            sent_ref[place] = own_ref[entries + entry]


def place_kernel(half, channels, rows_up, own_ref, other_ref, pick_ref, spread_ref, out_hbm, out_ref, imag, both, spread, out_sem):
    block = out_ref.shape[3]
    whole = rows_up - GROUP
    groups = channels * (rows_up // GROUP - 1) + (channels + 2) // 2
    at_row = lax.broadcasted_iota(jnp.int32, (rows_up, rows_up), 0)
    at_col = lax.broadcasted_iota(jnp.int32, (rows_up, rows_up), 1)
    back = lax.axis_index("slot") // (lax.axis_size("slot") // 4) % 2 == 1
    source = jnp.where(back, block - at_row, at_row)
    order = (source == at_col).astype(F32).astype(BF16)
    entries = out_ref.shape[1]
    for entry in range(entries):
        for at in range(0, imag.shape[2], LANES):
            value = jnp.zeros((GROUP, LANES), BF16)
            if entry < entries - 1:
                value += pick_ref[entry, 0] * other_ref[entries + entry, :, at : at + LANES]
            if entry > 0:
                value += pick_ref[entry, 1] * other_ref[entries + entry - 1, :, at : at + LANES]
            imag[entry, :, at : at + LANES] = value
    for part in range(2):
        for entry in range(entries):
            sides = []
            for mirrored in range(2):

                ref, first = ((own_ref, part * entries), (imag if part else other_ref, 0))[mirrored]

                def load(tile):
                    return ref[first + entry, :, tile * LANES : (tile + 1) * LANES]

                values = [unpack(load, g * half, half, GROUP).astype(F32) for g in range(groups)]
                sides.append(join_rows(values, channels, whole))
            for c in range(channels):
                at = (part * entries + entry) * channels + c
                value = jnp.concatenate([sides[0][c], sides[1][c]], axis=1)
                both[at * rows_up : (at + 1) * rows_up] = value.astype(BF16)
    for part in range(2):
        for entry in range(entries):
            for c in range(channels):
                at = (part * entries + entry) * channels + c
                value = jnp.dot(both[at * rows_up : (at + 1) * rows_up], spread_ref[part], preferred_element_type=F32)
                spread[:, at * LANES : (at + 1) * LANES] = value.astype(BF16)
    copies = []
    for part in range(2):
        for entry in range(entries):
            for c in range(channels):
                at = (part * entries + entry) * channels + c
                value = jnp.dot(order, spread[:, at * LANES : (at + 1) * LANES], preferred_element_type=F32)
                out_ref[part, entry, c] = value[:block, :block]
            copies.append(
                pltpu.make_async_copy(
                    out_ref.at[part, entry], out_hbm.at[part, entry], out_sem.at[part * entries + entry]
                )
            )
            copies[-1].start()
    for copy in copies:
        copy.wait()


def spread_table(block, half):
    table = np.zeros((2, 2 * LANES, LANES))
    for j in range(block):
        if j < half:
            table[:, j, j] = 1.0
        else:
            table[:, LANES + block - j, j] = (1.0, -1.0)
    return table.astype(ml_dtypes.bfloat16)


def up(value, unit):
    return -(-value // unit) * unit


def on_device(slots, parts, innovation, clear_mask, lag_list):
    _, channels, rows, cols = innovation.shape
    length = rows * parts
    block = cols // parts
    half = block // 2 + 1
    width = 2 * half
    entries = lag_list.shape[0]
    whole_vmem = pl.BlockSpec(memory_space=pltpu.VMEM)
    limit = pltpu.CompilerParams(vmem_limit_bytes=24 * 2**20)

    left_rows = up(channels * rows, GROUP)
    packed = up(left_rows // GROUP * width, LANES)
    pitch = 96
    table = column_table(cols, parts, half, pitch)
    whole = rows // GROUP
    order = [
        p * rows + a * GROUP + 2 * (b if a < whole else b % (GROUP // 4)) + parity
        for parity in range(2)
        for a in range(whole + 1)
        for p in range(parts)
        for b in range(GROUP // 2)
    ]
    ky_block = length // slots
    rows_up = up(ky_block + 1, GROUP)
    next_table = row_table(length, slots, rows_up, np.array(order))
    g, next_table = pl.pallas_call(
        functools.partial(column_kernel, width, pitch),
        in_specs=[pl.BlockSpec(memory_space=pl.ANY)] * 4,
        out_specs=[whole_vmem] * 2,
        out_shape=[pltpu.VMEM((parts, GROUP, packed), BF16), pltpu.VMEM(next_table.shape, BF16)],
        scratch_shapes=[
            pltpu.VMEM(innovation.shape[1:], BF16),
            pltpu.VMEM(clear_mask.shape[1:], jnp.int32),
            pltpu.VMEM(table.shape, BF16),
            pltpu.VMEM((channels, cols // LANES, rows, LANES), F32),
            pltpu.VMEM((2 * left_rows, cols), BF16),
            pltpu.VMEM((2 * left_rows, parts // 2 * pitch), F32),
            pltpu.SemaphoreType.DMA((channels,)),
            pltpu.SemaphoreType.DMA((channels,)),
            pltpu.SemaphoreType.DMA(()),
            pltpu.SemaphoreType.DMA(()),
        ],
        compiler_params=pltpu.CompilerParams(vmem_limit_bytes=55 * 2**20),
        name="columns",
    )(innovation, clear_mask, jnp.asarray(table), jnp.asarray(next_table))
    g = lax.all_to_all(g, "row", 0, 0, tiled=True)

    packed = 2 * up((channels * (rows_up // GROUP - 1) + (channels + 2) // 2) * half, LANES)
    f = pl.pallas_call(
        functools.partial(row_kernel, half, channels, rows_up),
        in_specs=[whole_vmem] * 2,
        out_specs=whole_vmem,
        out_shape=jax.ShapeDtypeStruct((slots, GROUP, packed), BF16),
        scratch_shapes=[pltpu.VMEM((2, next_table.shape[1] // 2, channels * LANES), BF16)],
        compiler_params=limit,
        name="rows",
    )(g, next_table)
    f = lax.all_to_all(f, "slot", 0, 0, tiled=True)

    own, sent, pick = pl.pallas_call(
        lag_kernel,
        in_specs=[pl.BlockSpec(memory_space=pl.ANY), whole_vmem],
        out_specs=[whole_vmem] * 3,
        out_shape=[
            jax.ShapeDtypeStruct((2 * entries, GROUP, packed // 2), BF16),
            jax.ShapeDtypeStruct((2 * entries - 1, GROUP, packed // 2), BF16),
            jax.ShapeDtypeStruct((entries, 2, GROUP, LANES), BF16),
        ],
        scratch_shapes=[
            pltpu.VMEM((slots, GROUP, packed), F32),
            pltpu.SMEM((entries,), jnp.int32),
            pltpu.SemaphoreType.DMA(()),
        ],
        compiler_params=limit,
        name="lags",
    )(lag_list, f)

    mirror = [
        (s * parts + p, (slots - 1 - s) * parts + parts - 1 - p) for s in range(slots) for p in range(parts)
    ]
    other = lax.ppermute(sent, ("slot", "row"), mirror)

    planes = 2 * entries * channels
    return pl.pallas_call(
        functools.partial(place_kernel, half, channels, rows_up),
        in_specs=[whole_vmem] * 4,
        out_specs=pl.BlockSpec(memory_space=pl.ANY),
        out_shape=jax.ShapeDtypeStruct((2, entries, channels, ky_block, block), F32),
        scratch_shapes=[
            pltpu.VMEM((2, entries, channels, ky_block, block), F32),
            pltpu.VMEM((entries, GROUP, packed // 2), BF16),
            pltpu.VMEM((planes * rows_up, 2 * LANES), BF16),
            pltpu.VMEM((rows_up, planes * LANES), BF16),
            pltpu.SemaphoreType.DMA((2 * entries,)),
        ],
        compiler_params=limit,
        name="place",
    )(own, other, pick, jnp.asarray(spread_table(block, half)))


def solution(mesh):
    placed = (P("slot", None, "row", None), P("slot", None, "row", None), P())
    return jax.shard_map(
        functools.partial(on_device, mesh.shape["slot"], mesh.shape["row"]),
        mesh=mesh,
        in_specs=placed,
        out_specs=P(None, None, None, "slot", "row"),
        check_vma=False,
    )
```

```python
import functools
import math

import jax
import jax.numpy as jnp
import ml_dtypes
import numpy as np
from jax import lax
from jax.experimental import pallas as pl
from jax.experimental.pallas import tpu as pltpu
from jax.sharding import PartitionSpec as P

F32 = jnp.float32
BF16 = jnp.bfloat16
LANES = 128
GROUP = 16


def phase(numbers, length):
    return (numbers % length) * (2.0 * math.pi / length)


def column_table(length, parts, half, pitch):
    block = length // parts
    kx = np.arange(parts // 2)[:, None] * block + np.arange(half)[None, :]
    angles = phase(np.arange(length)[:, None, None] * kx[None], length)
    table = np.zeros((length, parts // 2, pitch))
    table[:, :, :half] = np.cos(angles)
    table[:, :, half : 2 * half] = -np.sin(angles)
    return (table / math.sqrt(length)).reshape(length, parts // 2 * pitch).astype(ml_dtypes.bfloat16)


def row_table(length, parts, rows_up, row_order):
    block = length // parts
    ky = np.arange(parts // 4)[:, None] * block + np.arange(block + 1)[None, :]
    angles = phase(ky[:, :, None] * row_order[None, None, :], length)
    table = np.zeros((parts // 4, 2, rows_up, row_order.size))
    table[:, 0, : block + 1] = np.cos(angles)
    table[:, 1, : block + 1] = np.sin(angles)
    return (table / math.sqrt(length)).reshape(-1, row_order.size).astype(ml_dtypes.bfloat16)


def lane_index(shape):
    return lax.broadcasted_iota(jnp.int32, shape, len(shape) - 1)


class Packed:
    def __init__(self, tiles):
        self.tiles = [jnp.zeros((GROUP, LANES), F32) for _ in range(tiles)]
        self.lane = lane_index((GROUP, LANES))

    def put(self, value, start, width):
        tile, shift = divmod(start, LANES)
        inside = self.lane >= shift
        if shift + width <= LANES:
            inside &= self.lane < shift + width
        else:
            after = self.lane < shift + width - LANES
            self.tiles[tile + 1] = jnp.where(after, value, self.tiles[tile + 1])
        self.tiles[tile] = jnp.where(inside, value, self.tiles[tile])


def turn(value, lanes):
    lanes %= LANES
    return pltpu.roll(value, lanes, 1) if lanes else value


def unpack(load, start, width, rows):
    lane = lane_index((rows, LANES))
    tile, shift = divmod(start, LANES)
    value = load(tile)
    if shift + width > LANES:
        value = jnp.where(lane >= shift, value, load(tile + 1))
    return jnp.where(lane < width, turn(value, -shift), jnp.zeros((), BF16))


def column_kernel(
    width,
    pitch,
    x_hbm,
    mask_hbm,
    table_hbm,
    next_hbm,
    out_ref,
    next_ref,
    x,
    mask,
    table,
    wide,
    left,
    result,
    x_sem,
    mask_sem,
    table_sem,
    next_sem,
):
    channels, rows = x.shape[0], x.shape[1]
    parts, used = out_ref.shape[0], left.shape[0] // 2
    x_copies = [pltpu.make_async_copy(x_hbm.at[0, c], x.at[c], x_sem.at[c]) for c in range(channels)]
    mask_copies = [pltpu.make_async_copy(mask_hbm.at[0, c], mask.at[c], mask_sem.at[c]) for c in range(channels)]
    table_copy = pltpu.make_async_copy(table_hbm, table, table_sem)
    for c in range(channels):
        mask_copies[c].start()
        x_copies[c].start()
    table_copy.start()
    next_copy = pltpu.make_async_copy(next_hbm, next_ref, next_sem)
    next_copy.start()
    groups, eight = rows // GROUP, GROUP // 2
    tail = []

    def store(group, pieces):
        value = jnp.concatenate(pieces, axis=0)
        odd = lane_index(value.shape) % 2 == 1
        at = group * GROUP
        left[at : at + GROUP] = value.astype(BF16)
        left[used + at : used + at + GROUP] = jnp.where(odd, -value, value).astype(BF16)

    for c in range(channels):
        mask_copies[c].wait()
        x_copies[c].wait()
        for tile in range(wide.shape[1]):
            lanes = slice(tile * LANES, (tile + 1) * LANES)
            wide[c, tile] = x[c, :, lanes].astype(F32) * mask[c, :, lanes].astype(F32)

        def every_other(first, count):
            return jnp.concatenate([wide[c, tile, pl.ds(first, count, 2)] for tile in range(wide.shape[1])], axis=1)

        for a in range(groups):
            store(c * groups + a, [every_other(a * GROUP + parity, eight) for parity in range(2)])
        tail.append([every_other(groups * GROUP + parity, eight // 2) for parity in range(2)])
    if channels % 2:
        tail.append([jnp.zeros((eight // 2, left.shape[1]), F32)] * 2)
    for i in range(0, len(tail), 2):
        store(channels * groups + i // 2, [tail[i + side][parity] for parity in range(2) for side in range(2)])

    table_copy.wait()
    result[...] = jnp.dot(left[...], table[...], preferred_element_type=F32)

    lane = lane_index((GROUP, LANES))
    for k in range(parts // 2):
        tile, shift = divmod(k * pitch, LANES)
        for side in range(2):
            packed = Packed(out_ref.shape[2] // LANES)
            for g in range(used // GROUP):
                at = slice(side * used + g * GROUP, side * used + (g + 1) * GROUP)
                value = result[at, tile * LANES : (tile + 1) * LANES]
                if shift + width > LANES:
                    value = jnp.where(lane >= shift, value, result[at, (tile + 1) * LANES : (tile + 2) * LANES])
                packed.put(turn(value, g * width - shift), g * width, width)
            out_ref[side * (parts // 2) + k] = jnp.concatenate(packed.tiles, axis=1).astype(BF16)
    next_copy.wait()


def split_rows(blocks, whole):
    groups = [v[a : a + GROUP] for v in blocks for a in range(0, whole, GROUP)]
    tail = [v[whole : whole + 8] for v in blocks]
    last = blocks[0][whole + 8 : whole + 16]
    for c in range(1, len(blocks)):
        last = last + pltpu.roll(blocks[c][whole + 8 : whole + 16], c, 0)
    tail.append(last)
    return groups + [jnp.concatenate(tail[i : i + 2], axis=0) for i in range(0, len(tail), 2)]


def join_rows(groups, channels, whole):
    per = whole // GROUP
    tail = []
    for value in groups[channels * per :]:
        tail += [value[:8], value[8:]]
    blocks = []
    for c in range(channels):
        last = pltpu.roll(tail[channels], 8 - c, 0) if c else tail[channels]
        blocks.append(jnp.concatenate(groups[c * per : (c + 1) * per] + [tail[c], last], axis=0))
    return blocks


def row_kernel(half, channels, rows_up, x_ref, table_ref, out_ref, right):
    width = 2 * half
    parts = x_ref.shape[0]
    depth = parts * GROUP
    eight = depth // 2
    steps = right.shape[1] // eight
    tiles = out_ref.shape[2] // LANES // 2

    def load(tile):
        return x_ref[:, :, tile * LANES : (tile + 1) * LANES].reshape(depth, LANES)

    row_in_half = lax.broadcasted_iota(jnp.int32, (eight, LANES), 0) % (GROUP // 2)

    for c in range(channels):
        for a in range(steps):
            last = a == steps - 1
            group = channels * (steps - 1) + c // 2 if last else c * (steps - 1) + a
            value = unpack(load, group * width, width, depth).astype(F32)
            value = value.reshape(parts, 2, GROUP // 2, LANES)
            for parity in range(2):
                half_rows = value[:, parity].reshape(eight, LANES)
                if last:
                    half_rows = jnp.where((row_in_half >= GROUP // 4) == (c % 2 == 1), half_rows, 0.0)
                right[parity, a * eight : (a + 1) * eight, c * LANES : (c + 1) * LANES] = half_rows.astype(BF16)

    slots, depth_all = out_ref.shape[0], right.shape[1]
    for q in range(slots // 4):
        rows_here = slice(2 * q * rows_up, 2 * (q + 1) * rows_up)
        sums = [
            jnp.dot(
                table_ref[rows_here, parity * depth_all : (parity + 1) * depth_all],
                right[parity],
                preferred_element_type=F32,
            )
            for parity in range(2)
        ]
        for shifted in range(2):
            result = sums[0] - sums[1] if shifted else sums[0] + sums[1]
            sides = []
            for at in (0, rows_up):
                lanes = [slice(c * LANES, (c + 1) * LANES) for c in range(channels)]
                sides.append(split_rows([result[at : at + rows_up, l] for l in lanes], rows_up - GROUP))
            out = [Packed(tiles) for _ in range(4)]
            for g, (even, odd) in enumerate(zip(*sides)):
                start = g * half
                real_even, real_odd = turn(even, start), turn(odd, start - half)
                imag_even, imag_odd = turn(even, start - half), turn(odd, start)
                out[0].put(real_even + real_odd, start, half)
                out[1].put(imag_even - imag_odd, start, half)
                out[2].put(real_even - real_odd, start, half)
                out[3].put(imag_even + imag_odd, start, half)
            place = q + shifted * (slots // 2)
            for at, values in ((place, out[:2]), (slots - 1 - place, out[2:])):
                joined = jnp.concatenate(values[0].tiles + values[1].tiles, axis=1)
                out_ref[at] = joined.astype(BF16)


def entry_of(lag_ref, entries, lag):
    found = entries - 1
    for entry in reversed(range(entries - 1)):
        found = jnp.where(lag_ref[entry] == lag, entry, found)
    return found


def lag_kernel(lag_hbm, z_ref, own_ref, sent_ref, pick_ref, wide, known, lag_ref, lag_sem):
    slots, rows, lanes = z_ref.shape
    middle = lanes // 2
    entries = own_ref.shape[0] // 2
    lag_copy = pltpu.make_async_copy(lag_hbm, lag_ref, lag_sem)
    lag_copy.start()
    for at in range(0, middle, LANES):
        tile, other = slice(at, at + LANES), slice(middle + at, middle + at + LANES)
        values = []
        for t in range(slots):
            values.append((z_ref[t, :, tile].astype(F32), z_ref[t, :, other].astype(F32)))
            wide[t, :, tile], wide[t, :, other] = values[t]
        total = values[0][0] * values[0][0] + values[0][1] * values[0][1]
        for real, imag in values[1:]:
            total = total + (real * real + imag * imag)
        early, late = values[0], values[-1]
        known[0, :, tile] = (total * (1.0 / slots)).astype(BF16)
        known[1, :, tile] = (early[0] * late[0] + early[1] * late[1]).astype(BF16)
        known[2, :, tile] = (early[1] * late[0] - early[0] * late[1]).astype(BF16)
    lag_copy.wait()
    still, longest = entry_of(lag_ref, entries, 0), entry_of(lag_ref, entries, slots - 1)

    def place(entry):
        return entries + entry - jnp.where(entry > still, 1, 0)

    own_ref[still] = known[0]
    sent_ref[still] = known[0]
    own_ref[entries + still] = jnp.zeros((rows, middle), BF16)
    own_ref[longest] = known[1]
    sent_ref[longest] = known[1]
    own_ref[entries + longest] = known[2]
    sent_ref[place(longest)] = known[2]
    for entry in range(entries):
        for earlier, here in enumerate((entry < still, entry > still)):
            pick_ref[entry, earlier] = jnp.broadcast_to(jnp.where(here, 1.0, 0.0), pick_ref.shape[2:]).astype(BF16)

        @pl.when((entry != still) & (entry != longest))
        def _():
            lag = lag_ref[entry]

            def add(t, sums):
                early_real, early_imag = wide[t, :, :middle], wide[t, :, middle:]
                late_real, late_imag = wide[t + lag, :, :middle], wide[t + lag, :, middle:]
                return (
                    sums[0] + (early_real * late_real + early_imag * late_imag),
                    sums[1] + (early_imag * late_real - early_real * late_imag),
                )

            zero = jnp.zeros((rows, middle), F32)
            count = slots - lag
            sums = lax.fori_loop(0, count // 2, lambda i, sums: add(2 * i + 1, add(2 * i, sums)), (zero, zero))
            sums = lax.fori_loop(count // 2 * 2, count, add, sums)
            scale = 1.0 / jnp.broadcast_to(count.astype(F32), (rows, LANES))
            for at in range(0, middle, LANES):
                tile = slice(at, at + LANES)
                real, imag = [(value[:, tile] * scale).astype(BF16) for value in sums]
                own_ref[entry, :, tile], own_ref[entries + entry, :, tile] = real, imag
                sent_ref[entry, :, tile], sent_ref[place(entry), :, tile] = real, imag


def place_kernel(half, channels, rows_up, own_ref, other_ref, pick_ref, spread_ref, out_hbm, out_ref, imag, both, spread, out_sem):
    block = out_ref.shape[3]
    whole = rows_up - GROUP
    groups = channels * (rows_up // GROUP - 1) + (channels + 2) // 2
    at_row = lax.broadcasted_iota(jnp.int32, (rows_up, rows_up), 0)
    at_col = lax.broadcasted_iota(jnp.int32, (rows_up, rows_up), 1)
    back = lax.axis_index("slot") // (lax.axis_size("slot") // 4) % 2 == 1
    source = jnp.where(back, block - at_row, at_row)
    order = (source == at_col).astype(F32).astype(BF16)
    entries = out_ref.shape[1]
    for entry in range(entries):
        for at in range(0, imag.shape[2], LANES):
            value = jnp.zeros((GROUP, LANES), BF16)
            if entry < entries - 1:
                value += pick_ref[entry, 0] * other_ref[entries + entry, :, at : at + LANES]
            if entry > 0:
                value += pick_ref[entry, 1] * other_ref[entries + entry - 1, :, at : at + LANES]
            imag[entry, :, at : at + LANES] = value
    for part in range(2):
        for entry in range(entries):
            sides = []
            for mirrored in range(2):

                ref, first = ((own_ref, part * entries), (imag if part else other_ref, 0))[mirrored]

                def load(tile):
                    return ref[first + entry, :, tile * LANES : (tile + 1) * LANES]

                values = [unpack(load, g * half, half, GROUP).astype(F32) for g in range(groups)]
                sides.append(join_rows(values, channels, whole))
            for c in range(channels):
                at = (part * entries + entry) * channels + c
                value = jnp.concatenate([sides[0][c], sides[1][c]], axis=1)
                both[at * rows_up : (at + 1) * rows_up] = value.astype(BF16)
    for part in range(2):
        for entry in range(entries):
            for c in range(channels):
                at = (part * entries + entry) * channels + c
                value = jnp.dot(both[at * rows_up : (at + 1) * rows_up], spread_ref[part], preferred_element_type=F32)
                spread[:, at * LANES : (at + 1) * LANES] = value.astype(BF16)
    copies = []
    for part in range(2):
        for entry in range(entries):
            for c in range(channels):
                at = (part * entries + entry) * channels + c
                value = jnp.dot(order, spread[:, at * LANES : (at + 1) * LANES], preferred_element_type=F32)
                out_ref[part, entry, c] = value[:block, :block]
            copies.append(
                pltpu.make_async_copy(
                    out_ref.at[part, entry], out_hbm.at[part, entry], out_sem.at[part * entries + entry]
                )
            )
            copies[-1].start()
    for copy in copies:
        copy.wait()


def spread_table(block, half):
    table = np.zeros((2, 2 * LANES, LANES))
    for j in range(block):
        if j < half:
            table[:, j, j] = 1.0
        else:
            table[:, LANES + block - j, j] = (1.0, -1.0)
    return table.astype(ml_dtypes.bfloat16)


def up(value, unit):
    return -(-value // unit) * unit


def on_device(slots, parts, innovation, clear_mask, lag_list):
    _, channels, rows, cols = innovation.shape
    length = rows * parts
    block = cols // parts
    half = block // 2 + 1
    width = 2 * half
    entries = lag_list.shape[0]
    whole_vmem = pl.BlockSpec(memory_space=pltpu.VMEM)
    limit = pltpu.CompilerParams(vmem_limit_bytes=24 * 2**20)

    left_rows = up(channels * rows, GROUP)
    packed = up(left_rows // GROUP * width, LANES)
    pitch = 96
    table = column_table(cols, parts, half, pitch)
    whole = rows // GROUP
    order = [
        p * rows + a * GROUP + 2 * (b if a < whole else b % (GROUP // 4)) + parity
        for parity in range(2)
        for a in range(whole + 1)
        for p in range(parts)
        for b in range(GROUP // 2)
    ]
    ky_block = length // slots
    rows_up = up(ky_block + 1, GROUP)
    next_table = row_table(length, slots, rows_up, np.array(order))
    g, next_table = pl.pallas_call(
        functools.partial(column_kernel, width, pitch),
        in_specs=[pl.BlockSpec(memory_space=pl.ANY)] * 4,
        out_specs=[whole_vmem] * 2,
        out_shape=[pltpu.VMEM((parts, GROUP, packed), BF16), pltpu.VMEM(next_table.shape, BF16)],
        scratch_shapes=[
            pltpu.VMEM(innovation.shape[1:], BF16),
            pltpu.VMEM(clear_mask.shape[1:], jnp.int32),
            pltpu.VMEM(table.shape, BF16),
            pltpu.VMEM((channels, cols // LANES, rows, LANES), F32),
            pltpu.VMEM((2 * left_rows, cols), BF16),
            pltpu.VMEM((2 * left_rows, parts // 2 * pitch), F32),
            pltpu.SemaphoreType.DMA((channels,)),
            pltpu.SemaphoreType.DMA((channels,)),
            pltpu.SemaphoreType.DMA(()),
            pltpu.SemaphoreType.DMA(()),
        ],
        compiler_params=pltpu.CompilerParams(vmem_limit_bytes=55 * 2**20),
        name="columns",
    )(innovation, clear_mask, jnp.asarray(table), jnp.asarray(next_table))
    g = lax.all_to_all(g, "row", 0, 0, tiled=True)

    packed = 2 * up((channels * (rows_up // GROUP - 1) + (channels + 2) // 2) * half, LANES)
    f = pl.pallas_call(
        functools.partial(row_kernel, half, channels, rows_up),
        in_specs=[whole_vmem] * 2,
        out_specs=whole_vmem,
        out_shape=jax.ShapeDtypeStruct((slots, GROUP, packed), BF16),
        scratch_shapes=[pltpu.VMEM((2, next_table.shape[1] // 2, channels * LANES), BF16)],
        compiler_params=limit,
        name="rows",
    )(g, next_table)
    f = lax.all_to_all(f, "slot", 0, 0, tiled=True)

    own, sent, pick = pl.pallas_call(
        lag_kernel,
        in_specs=[pl.BlockSpec(memory_space=pl.ANY), whole_vmem],
        out_specs=[whole_vmem] * 3,
        out_shape=[
            jax.ShapeDtypeStruct((2 * entries, GROUP, packed // 2), BF16),
            jax.ShapeDtypeStruct((2 * entries - 1, GROUP, packed // 2), BF16),
            jax.ShapeDtypeStruct((entries, 2, GROUP, LANES), BF16),
        ],
        scratch_shapes=[
            pltpu.VMEM((slots, GROUP, packed), F32),
            pltpu.VMEM((3, GROUP, packed // 2), BF16),
            pltpu.SMEM((entries,), jnp.int32),
            pltpu.SemaphoreType.DMA(()),
        ],
        compiler_params=limit,
        name="lags",
    )(lag_list, f)

    mirror = [
        (s * parts + p, (slots - 1 - s) * parts + parts - 1 - p) for s in range(slots) for p in range(parts)
    ]
    other = lax.ppermute(sent, ("slot", "row"), mirror)

    planes = 2 * entries * channels
    return pl.pallas_call(
        functools.partial(place_kernel, half, channels, rows_up),
        in_specs=[whole_vmem] * 4,
        out_specs=pl.BlockSpec(memory_space=pl.ANY),
        out_shape=jax.ShapeDtypeStruct((2, entries, channels, ky_block, block), F32),
        scratch_shapes=[
            pltpu.VMEM((2, entries, channels, ky_block, block), F32),
            pltpu.VMEM((entries, GROUP, packed // 2), BF16),
            pltpu.VMEM((planes * rows_up, 2 * LANES), BF16),
            pltpu.VMEM((rows_up, planes * LANES), BF16),
            pltpu.SemaphoreType.DMA((2 * entries,)),
        ],
        compiler_params=limit,
        name="place",
    )(own, other, pick, jnp.asarray(spread_table(block, half)))


def solution(mesh):
    placed = (P("slot", None, "row", None), P("slot", None, "row", None), P())
    return jax.shard_map(
        functools.partial(on_device, mesh.shape["slot"], mesh.shape["row"]),
        mesh=mesh,
        in_specs=placed,
        out_specs=P(None, None, None, "slot", "row"),
        check_vma=False,
    )
```

```python
import functools
import math

import jax
import jax.numpy as jnp
import ml_dtypes
import numpy as np
from jax import lax
from jax.experimental import pallas as pl
from jax.experimental.pallas import tpu as pltpu
from jax.sharding import PartitionSpec as P

F32 = jnp.float32
BF16 = jnp.bfloat16
LANES = 128
GROUP = 16


def phase(numbers, length):
    return (numbers % length) * (2.0 * math.pi / length)


def column_table(length, parts, half, pitch):
    block = length // parts
    kx = np.arange(parts // 2)[:, None] * block + np.arange(half)[None, :]
    angles = phase(np.arange(length)[:, None, None] * kx[None], length)
    table = np.zeros((length, parts // 2, pitch))
    table[:, :, :half] = np.cos(angles)
    table[:, :, half : 2 * half] = -np.sin(angles)
    table = (table / math.sqrt(length)).reshape(length, parts // 2 * pitch)
    split = np.zeros((2, up(length, 2 * LANES) // 2, parts // 2 * pitch))
    for parity in range(2):
        split[parity, : length // 2] = table[parity::2]
    return split.astype(ml_dtypes.bfloat16)


def row_table(length, parts, rows_up, row_order):
    block = length // parts
    ky = np.arange(parts // 4)[:, None] * block + np.arange(block + 1)[None, :]
    angles = phase(ky[:, :, None] * row_order[None, None, :], length)
    table = np.zeros((parts // 4, 2, rows_up, row_order.size))
    table[:, 0, : block + 1] = np.cos(angles)
    table[:, 1, : block + 1] = np.sin(angles)
    return (table / math.sqrt(length)).reshape(-1, row_order.size).astype(ml_dtypes.bfloat16)


def lane_index(shape):
    return lax.broadcasted_iota(jnp.int32, shape, len(shape) - 1)


class Packed:
    def __init__(self, tiles):
        self.tiles = [jnp.zeros((GROUP, LANES), F32) for _ in range(tiles)]
        self.lane = lane_index((GROUP, LANES))

    def put(self, value, start, width):
        tile, shift = divmod(start, LANES)
        inside = self.lane >= shift
        if shift + width <= LANES:
            inside &= self.lane < shift + width
        else:
            after = self.lane < shift + width - LANES
            self.tiles[tile + 1] = jnp.where(after, value, self.tiles[tile + 1])
        self.tiles[tile] = jnp.where(inside, value, self.tiles[tile])


def turn(value, lanes):
    lanes %= LANES
    return pltpu.roll(value, lanes, 1) if lanes else value


def unpack(load, start, width, rows):
    lane = lane_index((rows, LANES))
    tile, shift = divmod(start, LANES)
    value = load(tile)
    if shift + width > LANES:
        value = jnp.where(lane >= shift, value, load(tile + 1))
    return jnp.where(lane < width, turn(value, -shift), jnp.zeros((), BF16))


def column_kernel(
    width,
    pitch,
    x_hbm,
    mask_hbm,
    table_hbm,
    next_hbm,
    out_ref,
    next_ref,
    x,
    mask,
    table,
    wide,
    left,
    halves,
    split,
    result,
    x_sem,
    mask_sem,
    table_sem,
    next_sem,
):
    channels, rows = x.shape[0], x.shape[1]
    parts, used, cols = out_ref.shape[0], left.shape[0], x.shape[2]
    x_copies = [pltpu.make_async_copy(x_hbm.at[0, c], x.at[c], x_sem.at[c]) for c in range(channels)]
    mask_copies = [pltpu.make_async_copy(mask_hbm.at[0, c], mask.at[c], mask_sem.at[c]) for c in range(channels)]
    table_copy = pltpu.make_async_copy(table_hbm, table, table_sem)
    for c in range(channels):
        mask_copies[c].start()
        x_copies[c].start()
    table_copy.start()
    next_copy = pltpu.make_async_copy(next_hbm, next_ref, next_sem)
    next_copy.start()
    square = (2 * LANES, 2 * LANES)
    target = lane_index(square)
    source = target % LANES * 2 + target // LANES
    split[...] = (lax.broadcasted_iota(jnp.int32, square, 0) == source).astype(F32).astype(BF16)
    groups, eight = rows // GROUP, GROUP // 2
    tail = []

    def store(group, pieces):
        value = jnp.concatenate(pieces, axis=0)
        at = group * GROUP
        left[at : at + GROUP, :cols] = value.astype(BF16)

    if left.shape[1] > cols:
        left[:, cols:] = jnp.zeros((used, left.shape[1] - cols), BF16)

    for c in range(channels):
        mask_copies[c].wait()
        x_copies[c].wait()
        for tile in range(wide.shape[1]):
            lanes = slice(tile * LANES, (tile + 1) * LANES)
            wide[c, tile] = x[c, :, lanes].astype(F32) * mask[c, :, lanes].astype(F32)

        def every_other(first, count):
            return jnp.concatenate([wide[c, tile, pl.ds(first, count, 2)] for tile in range(wide.shape[1])], axis=1)

        for a in range(groups):
            store(c * groups + a, [every_other(a * GROUP + parity, eight) for parity in range(2)])
        tail.append([every_other(groups * GROUP + parity, eight // 2) for parity in range(2)])
    if channels % 2:
        tail.append([jnp.zeros((eight // 2, cols), F32)] * 2)
    for i in range(0, len(tail), 2):
        store(channels * groups + i // 2, [tail[i + side][parity] for parity in range(2) for side in range(2)])

    for tile in range(left.shape[1] // (2 * LANES)):
        value = left[:, 2 * tile * LANES : 2 * (tile + 1) * LANES]
        value = jnp.dot(value, split[...], preferred_element_type=F32).astype(BF16)
        for parity in range(2):
            halves[parity, :, tile * LANES : (tile + 1) * LANES] = value[:, parity * LANES : (parity + 1) * LANES]
    table_copy.wait()
    even, odd = [jnp.dot(halves[parity], table[parity], preferred_element_type=F32) for parity in range(2)]
    result[:used] = even + odd
    result[used:] = even - odd

    lane = lane_index((GROUP, LANES))
    for k in range(parts // 2):
        tile, shift = divmod(k * pitch, LANES)
        for side in range(2):
            packed = Packed(out_ref.shape[2] // LANES)
            for g in range(used // GROUP):
                at = slice(side * used + g * GROUP, side * used + (g + 1) * GROUP)
                value = result[at, tile * LANES : (tile + 1) * LANES]
                if shift + width > LANES:
                    value = jnp.where(lane >= shift, value, result[at, (tile + 1) * LANES : (tile + 2) * LANES])
                packed.put(turn(value, g * width - shift), g * width, width)
            out_ref[side * (parts // 2) + k] = jnp.concatenate(packed.tiles, axis=1).astype(BF16)
    next_copy.wait()


def split_rows(blocks, whole):
    groups = [v[a : a + GROUP] for v in blocks for a in range(0, whole, GROUP)]
    tail = [v[whole : whole + 8] for v in blocks]
    last = blocks[0][whole + 8 : whole + 16]
    for c in range(1, len(blocks)):
        last = last + pltpu.roll(blocks[c][whole + 8 : whole + 16], c, 0)
    tail.append(last)
    return groups + [jnp.concatenate(tail[i : i + 2], axis=0) for i in range(0, len(tail), 2)]


def join_rows(groups, channels, whole):
    per = whole // GROUP
    tail = []
    for value in groups[channels * per :]:
        tail += [value[:8], value[8:]]
    blocks = []
    for c in range(channels):
        last = pltpu.roll(tail[channels], 8 - c, 0) if c else tail[channels]
        blocks.append(jnp.concatenate(groups[c * per : (c + 1) * per] + [tail[c], last], axis=0))
    return blocks


def row_kernel(half, channels, rows_up, x_ref, table_ref, out_ref, right):
    width = 2 * half
    parts = x_ref.shape[0]
    depth = parts * GROUP
    eight = depth // 2
    steps = right.shape[1] // eight
    tiles = out_ref.shape[2] // LANES // 2

    def load(tile):
        return x_ref[:, :, tile * LANES : (tile + 1) * LANES].reshape(depth, LANES)

    row_in_half = lax.broadcasted_iota(jnp.int32, (eight, LANES), 0) % (GROUP // 2)

    for c in range(channels):
        for a in range(steps):
            last = a == steps - 1
            group = channels * (steps - 1) + c // 2 if last else c * (steps - 1) + a
            value = unpack(load, group * width, width, depth).astype(F32)
            value = value.reshape(parts, 2, GROUP // 2, LANES)
            for parity in range(2):
                half_rows = value[:, parity].reshape(eight, LANES)
                if last:
                    half_rows = jnp.where((row_in_half >= GROUP // 4) == (c % 2 == 1), half_rows, 0.0)
                right[parity, a * eight : (a + 1) * eight, c * LANES : (c + 1) * LANES] = half_rows.astype(BF16)

    slots, depth_all = out_ref.shape[0], right.shape[1]
    for q in range(slots // 4):
        rows_here = slice(2 * q * rows_up, 2 * (q + 1) * rows_up)
        sums = [
            jnp.dot(
                table_ref[rows_here, parity * depth_all : (parity + 1) * depth_all],
                right[parity],
                preferred_element_type=F32,
            )
            for parity in range(2)
        ]
        for shifted in range(2):
            result = sums[0] - sums[1] if shifted else sums[0] + sums[1]
            sides = []
            for at in (0, rows_up):
                lanes = [slice(c * LANES, (c + 1) * LANES) for c in range(channels)]
                sides.append(split_rows([result[at : at + rows_up, l] for l in lanes], rows_up - GROUP))
            out = [Packed(tiles) for _ in range(4)]
            for g, (even, odd) in enumerate(zip(*sides)):
                start = g * half
                real_even, real_odd = turn(even, start), turn(odd, start - half)
                imag_even, imag_odd = turn(even, start - half), turn(odd, start)
                out[0].put(real_even + real_odd, start, half)
                out[1].put(imag_even - imag_odd, start, half)
                out[2].put(real_even - real_odd, start, half)
                out[3].put(imag_even + imag_odd, start, half)
            place = q + shifted * (slots // 2)
            for at, values in ((place, out[:2]), (slots - 1 - place, out[2:])):
                joined = jnp.concatenate(values[0].tiles + values[1].tiles, axis=1)
                out_ref[at] = joined.astype(BF16)


def entry_of(lag_ref, entries, lag):
    found = entries - 1
    for entry in reversed(range(entries - 1)):
        found = jnp.where(lag_ref[entry] == lag, entry, found)
    return found


def lag_kernel(lag_hbm, z_ref, own_ref, sent_ref, pick_ref, wide, known, lag_ref, lag_sem):
    slots, rows, lanes = z_ref.shape
    middle = lanes // 2
    entries = own_ref.shape[0] // 2
    lag_copy = pltpu.make_async_copy(lag_hbm, lag_ref, lag_sem)
    lag_copy.start()
    for at in range(0, middle, LANES):
        tile, other = slice(at, at + LANES), slice(middle + at, middle + at + LANES)
        values = []
        for t in range(slots):
            values.append((z_ref[t, :, tile].astype(F32), z_ref[t, :, other].astype(F32)))
            wide[t, :, tile], wide[t, :, other] = values[t]
        total = values[0][0] * values[0][0] + values[0][1] * values[0][1]
        for real, imag in values[1:]:
            total = total + (real * real + imag * imag)
        early, late = values[0], values[-1]
        known[0, :, tile] = (total * (1.0 / slots)).astype(BF16)
        known[1, :, tile] = (early[0] * late[0] + early[1] * late[1]).astype(BF16)
        known[2, :, tile] = (early[1] * late[0] - early[0] * late[1]).astype(BF16)
    lag_copy.wait()
    still, longest = entry_of(lag_ref, entries, 0), entry_of(lag_ref, entries, slots - 1)

    def place(entry):
        return entries + entry - jnp.where(entry > still, 1, 0)

    own_ref[still] = known[0]
    sent_ref[still] = known[0]
    own_ref[entries + still] = jnp.zeros((rows, middle), BF16)
    own_ref[longest] = known[1]
    sent_ref[longest] = known[1]
    own_ref[entries + longest] = known[2]
    sent_ref[place(longest)] = known[2]
    for entry in range(entries):
        for earlier, here in enumerate((entry < still, entry > still)):
            pick_ref[entry, earlier] = jnp.broadcast_to(jnp.where(here, 1.0, 0.0), pick_ref.shape[2:]).astype(BF16)

        @pl.when((entry != still) & (entry != longest))
        def _():
            lag = lag_ref[entry]

            def add(t, sums):
                early_real, early_imag = wide[t, :, :middle], wide[t, :, middle:]
                late_real, late_imag = wide[t + lag, :, :middle], wide[t + lag, :, middle:]
                return (
                    sums[0] + (early_real * late_real + early_imag * late_imag),
                    sums[1] + (early_imag * late_real - early_real * late_imag),
                )

            zero = jnp.zeros((rows, middle), F32)
            count = slots - lag
            sums = lax.fori_loop(0, count // 2, lambda i, sums: add(2 * i + 1, add(2 * i, sums)), (zero, zero))
            sums = lax.fori_loop(count // 2 * 2, count, add, sums)
            scale = 1.0 / jnp.broadcast_to(count.astype(F32), (rows, LANES))
            for at in range(0, middle, LANES):
                tile = slice(at, at + LANES)
                real, imag = [(value[:, tile] * scale).astype(BF16) for value in sums]
                own_ref[entry, :, tile], own_ref[entries + entry, :, tile] = real, imag
                sent_ref[entry, :, tile], sent_ref[place(entry), :, tile] = real, imag


def place_kernel(half, channels, rows_up, own_ref, other_ref, pick_ref, spread_ref, out_hbm, out_ref, imag, both, spread, out_sem):
    block = out_ref.shape[3]
    whole = rows_up - GROUP
    groups = channels * (rows_up // GROUP - 1) + (channels + 2) // 2
    at_row = lax.broadcasted_iota(jnp.int32, (rows_up, rows_up), 0)
    at_col = lax.broadcasted_iota(jnp.int32, (rows_up, rows_up), 1)
    back = lax.axis_index("slot") // (lax.axis_size("slot") // 4) % 2 == 1
    source = jnp.where(back, block - at_row, at_row)
    order = (source == at_col).astype(F32).astype(BF16)
    entries = out_ref.shape[1]
    for entry in range(entries):
        for at in range(0, imag.shape[2], LANES):
            value = jnp.zeros((GROUP, LANES), BF16)
            if entry < entries - 1:
                value += pick_ref[entry, 0] * other_ref[entries + entry, :, at : at + LANES]
            if entry > 0:
                value += pick_ref[entry, 1] * other_ref[entries + entry - 1, :, at : at + LANES]
            imag[entry, :, at : at + LANES] = value
    for part in range(2):
        for entry in range(entries):
            sides = []
            for mirrored in range(2):

                ref, first = ((own_ref, part * entries), (imag if part else other_ref, 0))[mirrored]

                def load(tile):
                    return ref[first + entry, :, tile * LANES : (tile + 1) * LANES]

                values = [unpack(load, g * half, half, GROUP).astype(F32) for g in range(groups)]
                sides.append(join_rows(values, channels, whole))
            for c in range(channels):
                at = (part * entries + entry) * channels + c
                value = jnp.concatenate([sides[0][c], sides[1][c]], axis=1)
                both[at * rows_up : (at + 1) * rows_up] = value.astype(BF16)
    for part in range(2):
        for entry in range(entries):
            for c in range(channels):
                at = (part * entries + entry) * channels + c
                value = jnp.dot(both[at * rows_up : (at + 1) * rows_up], spread_ref[part], preferred_element_type=F32)
                spread[:, at * LANES : (at + 1) * LANES] = value.astype(BF16)
    copies = []
    for part in range(2):
        for entry in range(entries):
            for c in range(channels):
                at = (part * entries + entry) * channels + c
                value = jnp.dot(order, spread[:, at * LANES : (at + 1) * LANES], preferred_element_type=F32)
                out_ref[part, entry, c] = value[:block, :block]
            copies.append(
                pltpu.make_async_copy(
                    out_ref.at[part, entry], out_hbm.at[part, entry], out_sem.at[part * entries + entry]
                )
            )
            copies[-1].start()
    for copy in copies:
        copy.wait()


def spread_table(block, half):
    table = np.zeros((2, 2 * LANES, LANES))
    for j in range(block):
        if j < half:
            table[:, j, j] = 1.0
        else:
            table[:, LANES + block - j, j] = (1.0, -1.0)
    return table.astype(ml_dtypes.bfloat16)


def up(value, unit):
    return -(-value // unit) * unit


def on_device(slots, parts, innovation, clear_mask, lag_list):
    _, channels, rows, cols = innovation.shape
    length = rows * parts
    block = cols // parts
    half = block // 2 + 1
    width = 2 * half
    entries = lag_list.shape[0]
    whole_vmem = pl.BlockSpec(memory_space=pltpu.VMEM)
    limit = pltpu.CompilerParams(vmem_limit_bytes=24 * 2**20)

    left_rows = up(channels * rows, GROUP)
    packed = up(left_rows // GROUP * width, LANES)
    pitch = 96
    table = column_table(cols, parts, half, pitch)
    whole = rows // GROUP
    order = [
        p * rows + a * GROUP + 2 * (b if a < whole else b % (GROUP // 4)) + parity
        for parity in range(2)
        for a in range(whole + 1)
        for p in range(parts)
        for b in range(GROUP // 2)
    ]
    ky_block = length // slots
    rows_up = up(ky_block + 1, GROUP)
    next_table = row_table(length, slots, rows_up, np.array(order))
    g, next_table = pl.pallas_call(
        functools.partial(column_kernel, width, pitch),
        in_specs=[pl.BlockSpec(memory_space=pl.ANY)] * 4,
        out_specs=[whole_vmem] * 2,
        out_shape=[pltpu.VMEM((parts, GROUP, packed), BF16), pltpu.VMEM(next_table.shape, BF16)],
        scratch_shapes=[
            pltpu.VMEM(innovation.shape[1:], BF16),
            pltpu.VMEM(clear_mask.shape[1:], jnp.int32),
            pltpu.VMEM(table.shape, BF16),
            pltpu.VMEM((channels, cols // LANES, rows, LANES), F32),
            pltpu.VMEM((left_rows, up(cols, 2 * LANES)), BF16),
            pltpu.VMEM((2, left_rows, up(cols, 2 * LANES) // 2), BF16),
            pltpu.VMEM((2 * LANES, 2 * LANES), BF16),
            pltpu.VMEM((2 * left_rows, parts // 2 * pitch), F32),
            pltpu.SemaphoreType.DMA((channels,)),
            pltpu.SemaphoreType.DMA((channels,)),
            pltpu.SemaphoreType.DMA(()),
            pltpu.SemaphoreType.DMA(()),
        ],
        compiler_params=pltpu.CompilerParams(vmem_limit_bytes=55 * 2**20),
        name="columns",
    )(innovation, clear_mask, jnp.asarray(table), jnp.asarray(next_table))
    g = lax.all_to_all(g, "row", 0, 0, tiled=True)

    packed = 2 * up((channels * (rows_up // GROUP - 1) + (channels + 2) // 2) * half, LANES)
    f = pl.pallas_call(
        functools.partial(row_kernel, half, channels, rows_up),
        in_specs=[whole_vmem] * 2,
        out_specs=whole_vmem,
        out_shape=jax.ShapeDtypeStruct((slots, GROUP, packed), BF16),
        scratch_shapes=[pltpu.VMEM((2, next_table.shape[1] // 2, channels * LANES), BF16)],
        compiler_params=limit,
        name="rows",
    )(g, next_table)
    f = lax.all_to_all(f, "slot", 0, 0, tiled=True)

    own, sent, pick = pl.pallas_call(
        lag_kernel,
        in_specs=[pl.BlockSpec(memory_space=pl.ANY), whole_vmem],
        out_specs=[whole_vmem] * 3,
        out_shape=[
            jax.ShapeDtypeStruct((2 * entries, GROUP, packed // 2), BF16),
            jax.ShapeDtypeStruct((2 * entries - 1, GROUP, packed // 2), BF16),
            jax.ShapeDtypeStruct((entries, 2, GROUP, LANES), BF16),
        ],
        scratch_shapes=[
            pltpu.VMEM((slots, GROUP, packed), F32),
            pltpu.VMEM((3, GROUP, packed // 2), BF16),
            pltpu.SMEM((entries,), jnp.int32),
            pltpu.SemaphoreType.DMA(()),
        ],
        compiler_params=limit,
        name="lags",
    )(lag_list, f)

    mirror = [
        (s * parts + p, (slots - 1 - s) * parts + parts - 1 - p) for s in range(slots) for p in range(parts)
    ]
    other = lax.ppermute(sent, ("slot", "row"), mirror)

    planes = 2 * entries * channels
    return pl.pallas_call(
        functools.partial(place_kernel, half, channels, rows_up),
        in_specs=[whole_vmem] * 4,
        out_specs=pl.BlockSpec(memory_space=pl.ANY),
        out_shape=jax.ShapeDtypeStruct((2, entries, channels, ky_block, block), F32),
        scratch_shapes=[
            pltpu.VMEM((2, entries, channels, ky_block, block), F32),
            pltpu.VMEM((entries, GROUP, packed // 2), BF16),
            pltpu.VMEM((planes * rows_up, 2 * LANES), BF16),
            pltpu.VMEM((rows_up, planes * LANES), BF16),
            pltpu.SemaphoreType.DMA((2 * entries,)),
        ],
        compiler_params=limit,
        name="place",
    )(own, other, pick, jnp.asarray(spread_table(block, half)))


def solution(mesh):
    placed = (P("slot", None, "row", None), P("slot", None, "row", None), P())
    return jax.shard_map(
        functools.partial(on_device, mesh.shape["slot"], mesh.shape["row"]),
        mesh=mesh,
        in_specs=placed,
        out_specs=P(None, None, None, "slot", "row"),
        check_vma=False,
    )
```

```python
import functools
import math

import jax
import jax.numpy as jnp
import ml_dtypes
import numpy as np
from jax import lax
from jax.experimental import pallas as pl
from jax.experimental.pallas import tpu as pltpu
from jax.sharding import PartitionSpec as P

F32 = jnp.float32
BF16 = jnp.bfloat16
LANES = 128
GROUP = 16


def phase(numbers, length):
    return (numbers % length) * (2.0 * math.pi / length)


def column_table(length, parts, half, pitch):
    block = length // parts
    kx = np.arange(parts // 2)[:, None] * block + np.arange(half)[None, :]
    angles = phase(np.arange(length)[:, None, None] * kx[None], length)
    table = np.zeros((length, parts // 2, pitch))
    table[:, :, :half] = np.cos(angles)
    table[:, :, half : 2 * half] = -np.sin(angles)
    table = (table / math.sqrt(length)).reshape(length, parts // 2 * pitch)
    return np.stack([table[parity::2] for parity in range(2)]).astype(ml_dtypes.bfloat16)


def row_table(length, parts, rows_up, row_order):
    block = length // parts
    ky = np.arange(parts // 4)[:, None] * block + np.arange(block + 1)[None, :]
    angles = phase(ky[:, :, None] * row_order[None, None, :], length)
    table = np.zeros((parts // 4, 2, rows_up, row_order.size))
    table[:, 0, : block + 1] = np.cos(angles)
    table[:, 1, : block + 1] = np.sin(angles)
    return (table / math.sqrt(length)).reshape(-1, row_order.size).astype(ml_dtypes.bfloat16)


def lane_index(shape):
    return lax.broadcasted_iota(jnp.int32, shape, len(shape) - 1)


class Packed:
    def __init__(self, tiles):
        self.tiles = [jnp.zeros((GROUP, LANES), F32) for _ in range(tiles)]
        self.lane = lane_index((GROUP, LANES))

    def put(self, value, start, width):
        tile, shift = divmod(start, LANES)
        inside = self.lane >= shift
        if shift + width <= LANES:
            inside &= self.lane < shift + width
        else:
            after = self.lane < shift + width - LANES
            self.tiles[tile + 1] = jnp.where(after, value, self.tiles[tile + 1])
        self.tiles[tile] = jnp.where(inside, value, self.tiles[tile])


def turn(value, lanes):
    lanes %= LANES
    return pltpu.roll(value, lanes, 1) if lanes else value


def unpack(load, start, width, rows):
    lane = lane_index((rows, LANES))
    tile, shift = divmod(start, LANES)
    value = load(tile)
    if shift + width > LANES:
        value = jnp.where(lane >= shift, value, load(tile + 1))
    return jnp.where(lane < width, turn(value, -shift), jnp.zeros((), BF16))


def column_kernel(
    width,
    pitch,
    x_hbm,
    mask_hbm,
    table_hbm,
    next_hbm,
    out_ref,
    next_ref,
    x,
    mask,
    table,
    wide,
    left,
    halves,
    split,
    result,
    x_sem,
    mask_sem,
    table_sem,
    next_sem,
):
    channels, rows = x.shape[0], x.shape[1]
    parts, used, cols = out_ref.shape[0], left.shape[0], x.shape[2]
    x_copies = [pltpu.make_async_copy(x_hbm.at[0, c], x.at[c], x_sem.at[c]) for c in range(channels)]
    mask_copies = [pltpu.make_async_copy(mask_hbm.at[0, c], mask.at[c], mask_sem.at[c]) for c in range(channels)]
    filled = table_hbm.shape[1]
    table_copy = pltpu.make_async_copy(table_hbm, table.at[:, :filled], table_sem)
    for c in range(channels):
        mask_copies[c].start()
        x_copies[c].start()
    table_copy.start()
    next_copy = pltpu.make_async_copy(next_hbm, next_ref, next_sem)
    next_copy.start()
    if filled < table.shape[1]:
        table[:, filled:] = jnp.zeros((2, table.shape[1] - filled, table.shape[2]), BF16)
    square = (2 * LANES, 2 * LANES)
    target = lane_index(square)
    source = target % LANES * 2 + target // LANES
    split[...] = (lax.broadcasted_iota(jnp.int32, square, 0) == source).astype(F32).astype(BF16)
    groups, eight = rows // GROUP, GROUP // 2
    tail = []

    def store(group, pieces):
        value = jnp.concatenate(pieces, axis=0)
        at = group * GROUP
        left[at : at + GROUP, :cols] = value.astype(BF16)

    if left.shape[1] > cols:
        left[:, cols:] = jnp.zeros((used, left.shape[1] - cols), BF16)

    for c in range(channels):
        mask_copies[c].wait()
        x_copies[c].wait()
        for tile in range(wide.shape[1]):
            lanes = slice(tile * LANES, (tile + 1) * LANES)
            wide[c, tile] = x[c, :, lanes].astype(F32) * mask[c, :, lanes].astype(F32)

        def every_other(first, count):
            return jnp.concatenate([wide[c, tile, pl.ds(first, count, 2)] for tile in range(wide.shape[1])], axis=1)

        for a in range(groups):
            store(c * groups + a, [every_other(a * GROUP + parity, eight) for parity in range(2)])
        tail.append([every_other(groups * GROUP + parity, eight // 2) for parity in range(2)])
    if channels % 2:
        tail.append([jnp.zeros((eight // 2, cols), F32)] * 2)
    for i in range(0, len(tail), 2):
        store(channels * groups + i // 2, [tail[i + side][parity] for parity in range(2) for side in range(2)])

    for tile in range(left.shape[1] // (2 * LANES)):
        value = left[:, 2 * tile * LANES : 2 * (tile + 1) * LANES]
        value = jnp.dot(value, split[...], preferred_element_type=F32).astype(BF16)
        for parity in range(2):
            halves[parity, :, tile * LANES : (tile + 1) * LANES] = value[:, parity * LANES : (parity + 1) * LANES]
    table_copy.wait()
    even, odd = [jnp.dot(halves[parity], table[parity], preferred_element_type=F32) for parity in range(2)]
    result[:used] = even + odd
    result[used:] = even - odd

    lane = lane_index((GROUP, LANES))
    for k in range(parts // 2):
        tile, shift = divmod(k * pitch, LANES)
        for side in range(2):
            packed = Packed(out_ref.shape[2] // LANES)
            for g in range(used // GROUP):
                at = slice(side * used + g * GROUP, side * used + (g + 1) * GROUP)
                value = result[at, tile * LANES : (tile + 1) * LANES]
                if shift + width > LANES:
                    value = jnp.where(lane >= shift, value, result[at, (tile + 1) * LANES : (tile + 2) * LANES])
                packed.put(turn(value, g * width - shift), g * width, width)
            out_ref[side * (parts // 2) + k] = jnp.concatenate(packed.tiles, axis=1).astype(BF16)
    next_copy.wait()


def split_rows(blocks, whole):
    groups = [v[a : a + GROUP] for v in blocks for a in range(0, whole, GROUP)]
    tail = [v[whole : whole + 8] for v in blocks]
    last = blocks[0][whole + 8 : whole + 16]
    for c in range(1, len(blocks)):
        last = last + pltpu.roll(blocks[c][whole + 8 : whole + 16], c, 0)
    tail.append(last)
    return groups + [jnp.concatenate(tail[i : i + 2], axis=0) for i in range(0, len(tail), 2)]


def join_rows(groups, channels, whole):
    per = whole // GROUP
    tail = []
    for value in groups[channels * per :]:
        tail += [value[:8], value[8:]]
    blocks = []
    for c in range(channels):
        last = pltpu.roll(tail[channels], 8 - c, 0) if c else tail[channels]
        blocks.append(jnp.concatenate(groups[c * per : (c + 1) * per] + [tail[c], last], axis=0))
    return blocks


def row_kernel(half, channels, rows_up, x_ref, table_ref, out_ref, right):
    width = 2 * half
    parts = x_ref.shape[0]
    depth = parts * GROUP
    eight = depth // 2
    steps = right.shape[1] // eight
    tiles = out_ref.shape[2] // LANES // 2

    def load(tile):
        return x_ref[:, :, tile * LANES : (tile + 1) * LANES].reshape(depth, LANES)

    row_in_half = lax.broadcasted_iota(jnp.int32, (eight, LANES), 0) % (GROUP // 2)

    for c in range(channels):
        for a in range(steps):
            last = a == steps - 1
            group = channels * (steps - 1) + c // 2 if last else c * (steps - 1) + a
            value = unpack(load, group * width, width, depth).astype(F32)
            value = value.reshape(parts, 2, GROUP // 2, LANES)
            for parity in range(2):
                half_rows = value[:, parity].reshape(eight, LANES)
                if last:
                    half_rows = jnp.where((row_in_half >= GROUP // 4) == (c % 2 == 1), half_rows, 0.0)
                right[parity, a * eight : (a + 1) * eight, c * LANES : (c + 1) * LANES] = half_rows.astype(BF16)

    slots, depth_all = out_ref.shape[0], right.shape[1]
    for q in range(slots // 4):
        rows_here = slice(2 * q * rows_up, 2 * (q + 1) * rows_up)
        sums = [
            jnp.dot(
                table_ref[rows_here, parity * depth_all : (parity + 1) * depth_all],
                right[parity],
                preferred_element_type=F32,
            )
            for parity in range(2)
        ]
        for shifted in range(2):
            result = sums[0] - sums[1] if shifted else sums[0] + sums[1]
            sides = []
            for at in (0, rows_up):
                lanes = [slice(c * LANES, (c + 1) * LANES) for c in range(channels)]
                sides.append(split_rows([result[at : at + rows_up, l] for l in lanes], rows_up - GROUP))
            out = [Packed(tiles) for _ in range(4)]
            for g, (even, odd) in enumerate(zip(*sides)):
                start = g * half
                real_even, real_odd = turn(even, start), turn(odd, start - half)
                imag_even, imag_odd = turn(even, start - half), turn(odd, start)
                out[0].put(real_even + real_odd, start, half)
                out[1].put(imag_even - imag_odd, start, half)
                out[2].put(real_even - real_odd, start, half)
                out[3].put(imag_even + imag_odd, start, half)
            place = q + shifted * (slots // 2)
            for at, values in ((place, out[:2]), (slots - 1 - place, out[2:])):
                joined = jnp.concatenate(values[0].tiles + values[1].tiles, axis=1)
                out_ref[at] = joined.astype(BF16)


def entry_of(lag_ref, entries, lag):
    found = entries - 1
    for entry in reversed(range(entries - 1)):
        found = jnp.where(lag_ref[entry] == lag, entry, found)
    return found


def lag_kernel(lag_hbm, z_ref, own_ref, sent_ref, pick_ref, wide, known, lag_ref, lag_sem):
    slots, rows, lanes = z_ref.shape
    middle = lanes // 2
    entries = own_ref.shape[0] // 2
    lag_copy = pltpu.make_async_copy(lag_hbm, lag_ref, lag_sem)
    lag_copy.start()
    for at in range(0, middle, LANES):
        tile, other = slice(at, at + LANES), slice(middle + at, middle + at + LANES)
        values = []
        for t in range(slots):
            values.append((z_ref[t, :, tile].astype(F32), z_ref[t, :, other].astype(F32)))
            wide[t, :, tile], wide[t, :, other] = values[t]
        total = values[0][0] * values[0][0] + values[0][1] * values[0][1]
        for real, imag in values[1:]:
            total = total + (real * real + imag * imag)
        early, late = values[0], values[-1]
        known[0, :, tile] = (total * (1.0 / slots)).astype(BF16)
        known[1, :, tile] = (early[0] * late[0] + early[1] * late[1]).astype(BF16)
        known[2, :, tile] = (early[1] * late[0] - early[0] * late[1]).astype(BF16)
    lag_copy.wait()
    still, longest = entry_of(lag_ref, entries, 0), entry_of(lag_ref, entries, slots - 1)

    def place(entry):
        return entries + entry - jnp.where(entry > still, 1, 0)

    own_ref[still] = known[0]
    sent_ref[still] = known[0]
    own_ref[entries + still] = jnp.zeros((rows, middle), BF16)
    own_ref[longest] = known[1]
    sent_ref[longest] = known[1]
    own_ref[entries + longest] = known[2]
    sent_ref[place(longest)] = known[2]
    for entry in range(entries):
        for earlier, here in enumerate((entry < still, entry > still)):
            pick_ref[entry, earlier] = jnp.broadcast_to(jnp.where(here, 1.0, 0.0), pick_ref.shape[2:]).astype(BF16)

        @pl.when((entry != still) & (entry != longest))
        def _():
            lag = lag_ref[entry]

            def add(t, sums):
                early_real, early_imag = wide[t, :, :middle], wide[t, :, middle:]
                late_real, late_imag = wide[t + lag, :, :middle], wide[t + lag, :, middle:]
                return (
                    sums[0] + (early_real * late_real + early_imag * late_imag),
                    sums[1] + (early_imag * late_real - early_real * late_imag),
                )

            zero = jnp.zeros((rows, middle), F32)
            count = slots - lag
            sums = lax.fori_loop(0, count // 2, lambda i, sums: add(2 * i + 1, add(2 * i, sums)), (zero, zero))
            sums = lax.fori_loop(count // 2 * 2, count, add, sums)
            scale = 1.0 / jnp.broadcast_to(count.astype(F32), (rows, LANES))
            for at in range(0, middle, LANES):
                tile = slice(at, at + LANES)
                real, imag = [(value[:, tile] * scale).astype(BF16) for value in sums]
                own_ref[entry, :, tile], own_ref[entries + entry, :, tile] = real, imag
                sent_ref[entry, :, tile], sent_ref[place(entry), :, tile] = real, imag


def place_kernel(half, channels, rows_up, own_ref, other_ref, pick_ref, spread_ref, out_hbm, out_ref, imag, both, spread, out_sem):
    block = out_ref.shape[3]
    whole = rows_up - GROUP
    groups = channels * (rows_up // GROUP - 1) + (channels + 2) // 2
    at_row = lax.broadcasted_iota(jnp.int32, (rows_up, rows_up), 0)
    at_col = lax.broadcasted_iota(jnp.int32, (rows_up, rows_up), 1)
    back = lax.axis_index("slot") // (lax.axis_size("slot") // 4) % 2 == 1
    source = jnp.where(back, block - at_row, at_row)
    order = (source == at_col).astype(F32).astype(BF16)
    entries = out_ref.shape[1]
    for entry in range(entries):
        for at in range(0, imag.shape[2], LANES):
            value = jnp.zeros((GROUP, LANES), BF16)
            if entry < entries - 1:
                value += pick_ref[entry, 0] * other_ref[entries + entry, :, at : at + LANES]
            if entry > 0:
                value += pick_ref[entry, 1] * other_ref[entries + entry - 1, :, at : at + LANES]
            imag[entry, :, at : at + LANES] = value
    for part in range(2):
        for entry in range(entries):
            sides = []
            for mirrored in range(2):

                ref, first = ((own_ref, part * entries), (imag if part else other_ref, 0))[mirrored]

                def load(tile):
                    return ref[first + entry, :, tile * LANES : (tile + 1) * LANES]

                values = [unpack(load, g * half, half, GROUP).astype(F32) for g in range(groups)]
                sides.append(join_rows(values, channels, whole))
            for c in range(channels):
                at = (part * entries + entry) * channels + c
                value = jnp.concatenate([sides[0][c], sides[1][c]], axis=1)
                both[at * rows_up : (at + 1) * rows_up] = value.astype(BF16)
    for part in range(2):
        for entry in range(entries):
            for c in range(channels):
                at = (part * entries + entry) * channels + c
                value = jnp.dot(both[at * rows_up : (at + 1) * rows_up], spread_ref[part], preferred_element_type=F32)
                spread[:, at * LANES : (at + 1) * LANES] = value.astype(BF16)
    copies = []
    for part in range(2):
        for entry in range(entries):
            for c in range(channels):
                at = (part * entries + entry) * channels + c
                value = jnp.dot(order, spread[:, at * LANES : (at + 1) * LANES], preferred_element_type=F32)
                out_ref[part, entry, c] = value[:block, :block]
            copies.append(
                pltpu.make_async_copy(
                    out_ref.at[part, entry], out_hbm.at[part, entry], out_sem.at[part * entries + entry]
                )
            )
            copies[-1].start()
    for copy in copies:
        copy.wait()


def spread_table(block, half):
    table = np.zeros((2, 2 * LANES, LANES))
    for j in range(block):
        if j < half:
            table[:, j, j] = 1.0
        else:
            table[:, LANES + block - j, j] = (1.0, -1.0)
    return table.astype(ml_dtypes.bfloat16)


def up(value, unit):
    return -(-value // unit) * unit


def on_device(slots, parts, innovation, clear_mask, lag_list):
    _, channels, rows, cols = innovation.shape
    length = rows * parts
    block = cols // parts
    half = block // 2 + 1
    width = 2 * half
    entries = lag_list.shape[0]
    whole_vmem = pl.BlockSpec(memory_space=pltpu.VMEM)
    limit = pltpu.CompilerParams(vmem_limit_bytes=24 * 2**20)

    left_rows = up(channels * rows, GROUP)
    packed = up(left_rows // GROUP * width, LANES)
    pitch = 96
    table = column_table(cols, parts, half, pitch)
    whole = rows // GROUP
    order = [
        p * rows + a * GROUP + 2 * (b if a < whole else b % (GROUP // 4)) + parity
        for parity in range(2)
        for a in range(whole + 1)
        for p in range(parts)
        for b in range(GROUP // 2)
    ]
    ky_block = length // slots
    rows_up = up(ky_block + 1, GROUP)
    next_table = row_table(length, slots, rows_up, np.array(order))
    g, next_table = pl.pallas_call(
        functools.partial(column_kernel, width, pitch),
        in_specs=[pl.BlockSpec(memory_space=pl.ANY)] * 4,
        out_specs=[whole_vmem] * 2,
        out_shape=[pltpu.VMEM((parts, GROUP, packed), BF16), pltpu.VMEM(next_table.shape, BF16)],
        scratch_shapes=[
            pltpu.VMEM(innovation.shape[1:], BF16),
            pltpu.VMEM(clear_mask.shape[1:], jnp.int32),
            pltpu.VMEM((2, up(cols, 2 * LANES) // 2, table.shape[2]), BF16),
            pltpu.VMEM((channels, cols // LANES, rows, LANES), F32),
            pltpu.VMEM((left_rows, up(cols, 2 * LANES)), BF16),
            pltpu.VMEM((2, left_rows, up(cols, 2 * LANES) // 2), BF16),
            pltpu.VMEM((2 * LANES, 2 * LANES), BF16),
            pltpu.VMEM((2 * left_rows, parts // 2 * pitch), F32),
            pltpu.SemaphoreType.DMA((channels,)),
            pltpu.SemaphoreType.DMA((channels,)),
            pltpu.SemaphoreType.DMA(()),
            pltpu.SemaphoreType.DMA(()),
        ],
        compiler_params=pltpu.CompilerParams(vmem_limit_bytes=55 * 2**20),
        name="columns",
    )(innovation, clear_mask, jnp.asarray(table), jnp.asarray(next_table))
    g = lax.all_to_all(g, "row", 0, 0, tiled=True)

    packed = 2 * up((channels * (rows_up // GROUP - 1) + (channels + 2) // 2) * half, LANES)
    f = pl.pallas_call(
        functools.partial(row_kernel, half, channels, rows_up),
        in_specs=[whole_vmem] * 2,
        out_specs=whole_vmem,
        out_shape=jax.ShapeDtypeStruct((slots, GROUP, packed), BF16),
        scratch_shapes=[pltpu.VMEM((2, next_table.shape[1] // 2, channels * LANES), BF16)],
        compiler_params=limit,
        name="rows",
    )(g, next_table)
    f = lax.all_to_all(f, "slot", 0, 0, tiled=True)

    own, sent, pick = pl.pallas_call(
        lag_kernel,
        in_specs=[pl.BlockSpec(memory_space=pl.ANY), whole_vmem],
        out_specs=[whole_vmem] * 3,
        out_shape=[
            jax.ShapeDtypeStruct((2 * entries, GROUP, packed // 2), BF16),
            jax.ShapeDtypeStruct((2 * entries - 1, GROUP, packed // 2), BF16),
            jax.ShapeDtypeStruct((entries, 2, GROUP, LANES), BF16),
        ],
        scratch_shapes=[
            pltpu.VMEM((slots, GROUP, packed), F32),
            pltpu.VMEM((3, GROUP, packed // 2), BF16),
            pltpu.SMEM((entries,), jnp.int32),
            pltpu.SemaphoreType.DMA(()),
        ],
        compiler_params=limit,
        name="lags",
    )(lag_list, f)

    mirror = [
        (s * parts + p, (slots - 1 - s) * parts + parts - 1 - p) for s in range(slots) for p in range(parts)
    ]
    other = lax.ppermute(sent, ("slot", "row"), mirror)

    planes = 2 * entries * channels
    return pl.pallas_call(
        functools.partial(place_kernel, half, channels, rows_up),
        in_specs=[whole_vmem] * 4,
        out_specs=pl.BlockSpec(memory_space=pl.ANY),
        out_shape=jax.ShapeDtypeStruct((2, entries, channels, ky_block, block), F32),
        scratch_shapes=[
            pltpu.VMEM((2, entries, channels, ky_block, block), F32),
            pltpu.VMEM((entries, GROUP, packed // 2), BF16),
            pltpu.VMEM((planes * rows_up, 2 * LANES), BF16),
            pltpu.VMEM((rows_up, planes * LANES), BF16),
            pltpu.SemaphoreType.DMA((2 * entries,)),
        ],
        compiler_params=limit,
        name="place",
    )(own, other, pick, jnp.asarray(spread_table(block, half)))


def solution(mesh):
    placed = (P("slot", None, "row", None), P("slot", None, "row", None), P())
    return jax.shard_map(
        functools.partial(on_device, mesh.shape["slot"], mesh.shape["row"]),
        mesh=mesh,
        in_specs=placed,
        out_specs=P(None, None, None, "slot", "row"),
        check_vma=False,
    )
```
